32 devices in a mesh: gx: 4 (over z), gy: 8 (over y, x, core).
Axes of the slice: x: 2, y: 2, z: 4, core: 2. Of those that a mesh axis runs over, the one named last changes fastest.
Arguments:
- noise: float32 [4, 512, 512], P('gx', 'gy'), may hold values from -6 to 6
- stencil: float32 [9], replicated, may hold values from 0.04 to 0.2
- mean_counts: float32 [4], replicated, may hold values from 0.5 to 4
- bias_one: float32 [4], replicated, may hold values from 1 to 2
- bias_two: float32 [4], replicated, may hold values from 0.05 to 0.3
- owner: int32 [8, 4, 4, 1], P('gy', 'gx'), may hold values from 0 to 3; in each aligned block of 4 rows (0 to 3, 4 to 7, ..., all dimensions but the last counted through in order) at most 2 rows name the same one
- depth: int32 [4, 8, 8], P('gx', None, 'gy'), may hold values from 0 to 3
- counts: int32 [4, 8, 8, 64, 128], P('gx', None, 'gy'), may hold values from 0 to 6
Outputs:
- gradient: float32 [4, 512, 512], P('gx', 'gy')
- density: float32 [4, 512, 512], P('gx', 'gy')
The draws below stay inside these ranges and needn't reach their ends.
Inputs may be any that keep to these rules, and one draw needn't show every extreme that they name: Of the tiles of one device (aligned blocks of 4 rows), at most 2 name the same owner, and in every draw some owner is named exactly 2 times by one device.
All inputs are finite; a program needn't handle non-finite values.
Results may differ from the reference program's by a relative error of at most 0.0001.
Values sent between devices are 32-bit elements; how exact they have to be, the bound alone decides.
No kernel may reach another device: no remote copies, remote signals or barrier semaphores. Data moves between devices by JAX's collectives and lax.ppermute only.
A program may use at most 64 MiB of HBM per device.

```python
import math
import jax
import jax.numpy as jnp
import numpy as np
from jax import lax

NG = 512
TC = 128
DEPTHS = 4
PL = 4
XL = 64
NT = 4
TILES_DEV = 4
CAP = 2
SLOTS = 8
N_GX = 4
N_GY = 8


def place_ends(result, own_key, least, high):
    place = [jax.random.randint(jax.random.fold_in(own_key, axis), (), 0, length) for axis, length in enumerate(result.shape)]
    longest = result.shape.index(max(result.shape))
    beside = place[:longest] + [(place[longest] + 1) % result.shape[longest]] + place[longest + 1:]
    return result.at[tuple(place)].set(least).at[tuple(beside)].set(high)


def levels(stream_key, extent, cuts, smallest, high):
    def one(dim, parts):
        heights = jax.random.uniform(jax.random.fold_in(jax.random.fold_in(stream_key, 6), dim), (parts,), jnp.float32, smallest / len(cuts), high / len(cuts))
        return jnp.repeat(jnp.exp(heights), extent[dim] // parts).reshape((-1,) + (1,) * (len(extent) - dim - 1))

    level = one(*cuts[0])
    for cut in cuts[1:]:
        level = level * one(*cut)
    return level


def routed_block(key, own, number, rows, amount, top, bound, skew):
    ranking = jax.random.permutation(key, amount)
    heavy_load, common = portions_of(amount, rows * top, bound, skew, True), portions_of(amount, rows * top, bound, skew, False)
    places = jnp.arange(amount)

    def named(tallies, turn):
        used = int((tallies > 0).sum())
        fixed = max(1, used // 4)
        shifted = fixed + (places - fixed + turn * (used - fixed)) % max(1, amount - fixed)
        return jnp.zeros((amount,), jnp.int32).at[ranking[jnp.where(places < fixed, places, shifted)]].set(jnp.asarray(tallies, jnp.int32))

    tallies = jnp.where(number % 4 == 0, named(heavy_load, number // 4), named(common, number - number // 4 - 1))
    mixed = jax.random.permutation(jax.random.fold_in(own, 3), amount)
    donor, sink = mixed[0:amount // 2 * 2:2], mixed[1:amount // 2 * 2:2]
    slack = jnp.minimum(tallies[donor] - 1, bound - tallies[sink]) // 2
    slack = jnp.where((donor == ranking[0]) | (sink == ranking[0]) | (tallies[sink] == 0), 0, jnp.maximum(slack, 0))
    shifted = jax.random.randint(jax.random.fold_in(own, 4), (amount // 2,), 0, 1 << 20) % (slack + 1)
    tallies = tallies.at[donor].add(-shifted).at[sink].add(shifted)
    items = jnp.searchsorted(jnp.cumsum(tallies), jnp.arange(rows * top), side="right").astype(jnp.int32)
    grid = items.reshape(top, rows).T
    grid = grid[jax.random.permutation(jax.random.fold_in(own, 1), rows)]
    turn = jax.random.randint(jax.random.fold_in(own, 2), (rows, 1), 0, top)
    return jnp.take_along_axis(grid, (jnp.arange(top)[None, :] + turn) % top, axis=1)


def portions_of(number_of, total, limit, skew, full):
    loads = [(1 << 20) // math.isqrt(rank ** skew) + 1 for rank in range(1, number_of + 1)]
    largest = limit if full else min(limit, max(-(-total // number_of), total * loads[0] // sum(loads)))
    least = 1 if total - largest >= number_of - 1 else 0
    holding, rest = [largest] + [least] * (number_of - 1), total - largest - least * (number_of - 1)
    while rest > 0:
        candidates = [i for i in range(1, number_of) if holding[i] < largest] or [i for i in range(1, number_of) if holding[i] < limit]
        whole, remaining = sum([loads[i] for i in candidates]), rest
        for i in candidates:
            more = min(limit - holding[i], max(1, remaining * loads[i] // whole), rest)
            holding[i] = holding[i] + more
            rest = rest - more
    return np.array(holding)


def centred(key, extent, deviation, reach, split=(), held_as=jnp.bfloat16):
    drawn = jax.random.normal(key, extent, jnp.float32) * deviation
    if len(split) > 0:
        drawn = levels(key, extent, split, -0.22, 0.18) * drawn
    return jnp.clip(drawn, min=-reach, max=reach).astype(held_as)


def setup_inputs(seed: int = 0) -> dict:
    streams_of = jax.random.split(jax.random.key(seed), 9)
    noise = centred(streams_of[0], (PL, NG, NG), 1.0, 6.0, ((0, 4), (1, 8)), jnp.float32)
    stencil = jnp.clip(jax.random.uniform(streams_of[1], (9,), jnp.float32, 0.04, 0.2), 0.04, 0.2)
    mean_counts = jnp.clip(jnp.exp(jax.random.uniform(streams_of[2], (DEPTHS,), jnp.float32, math.log(0.5), math.log(4.0))), 0.5, 4.0)
    bias_one = jnp.clip(jax.random.uniform(streams_of[3], (DEPTHS,), jnp.float32, 1.0, 2.0), 1.0, 2.0)
    bias_two = jnp.clip(jax.random.uniform(streams_of[4], (DEPTHS,), jnp.float32, 0.05, 0.3), 0.05, 0.3)
    owner_keys = jax.random.split(jax.random.fold_in(streams_of[5], 1), N_GY * PL * NT // TILES_DEV)
    owner_turns = jax.random.permutation(jax.random.fold_in(streams_of[5], 3), N_GY * PL * NT // TILES_DEV)
    owner = jax.vmap(lambda own, number: routed_block(jax.random.fold_in(streams_of[5], 2), own, number, TILES_DEV, N_GX, 1, CAP, 2))(owner_keys, owner_turns).reshape((N_GY, PL, NT, 1))
    depth = place_ends(jax.random.randint(streams_of[6], (N_GX, SLOTS, N_GY), 0, DEPTHS), jax.random.fold_in(streams_of[6], 1), 0, DEPTHS - 1).astype(jnp.int32)
    counts = place_ends(jax.random.randint(streams_of[7], (N_GX, SLOTS, N_GY, XL, TC), 0, 7), jax.random.fold_in(streams_of[7], 1), 0, 6).astype(jnp.int32)
    return {"noise": noise, "stencil": stencil, "mean_counts": mean_counts, "bias_one": bias_one, "bias_two": bias_two, "owner": owner, "depth": depth, "counts": counts}


AMPLITUDE = 0.75
PIVOT = 1.0
GROWTH = 7.0 / 8.0

def spectra_tables():
    steps_all = jnp.fft.fftfreq(NG) * NG
    wave_x = 2.0 * math.pi / NG * steps_all[:, None]
    wave_y = 2.0 * math.pi / NG * steps_all[None, :]
    wave_sq = wave_x * wave_x + wave_y * wave_y
    keep_mask = (jnp.abs(steps_all)[:, None] * 2 != NG) & (jnp.abs(steps_all)[None, :] * 2 != NG)
    wave_safe = jnp.where(wave_sq > 0, wave_sq, 1.0)
    inverse_sq = jnp.where(wave_sq > 0, 1.0 / wave_safe, 0.0)
    envelope = jnp.where(keep_mask, AMPLITUDE * (jnp.sqrt(wave_sq) / PIVOT) / (1.0 + wave_sq / (PIVOT * PIVOT)), 0.0)
    factors = [jnp.ones_like(wave_sq), wave_x * inverse_sq, wave_y * inverse_sq, wave_x, wave_y]
    return (envelope, factors)

def stencil_sum(field, weights, orient):
    summed = jnp.zeros_like(field)
    for step_x in (-1, 0, 1):
        for step_y in (-1, 0, 1):
            summed = summed + weights[(step_x + 1) * 3 + step_y + 1] * jnp.roll(field, (-orient * step_x, -orient * step_y), axis=(1, 2))
    return summed

def reference(noise, stencil, mean_counts, bias_one, bias_two, owner, depth, counts):
    envelope, factors = spectra_tables()
    wave_modes = jnp.fft.fft2(noise, axes=(1, 2)) * envelope
    fields = []
    for field_index in range(5):
        if field_index == 0:
            spectrum = wave_modes
        else:
            spectrum = 1j * factors[field_index] * wave_modes
        fields.append(jnp.real(jnp.fft.ifft2(spectrum, axes=(1, 2))).astype(jnp.float32))
    linear, shift_x, shift_y, slope_x, slope_y = fields
    density = linear + GROWTH * linear * linear - (shift_x * slope_x + shift_y * slope_y)
    smooth = stencil_sum(density, stencil, 1)
    tile_vals = smooth.reshape(PL, N_GY, XL, NT, TC).transpose(1, 0, 3, 2, 4).reshape(N_GY, N_GX, TILES_DEV, XL, TC)
    dest_owner = owner.reshape(N_GY, N_GX, TILES_DEV)
    onehot = (dest_owner[..., None] == jnp.arange(N_GX, dtype=jnp.int32)).astype(jnp.int32)
    rank_in = lax.optimization_barrier(jnp.sum((jnp.cumsum(onehot, axis=2) - onehot) * onehot, axis=3))
    slot_index = jnp.arange(N_GX, dtype=jnp.int32)[None, :, None] * CAP + rank_in
    column = jnp.broadcast_to(jnp.arange(N_GY, dtype=jnp.int32)[:, None, None], dest_owner.shape)
    cell_counts = counts[dest_owner, slot_index, column].astype(jnp.float32)
    classes = depth[dest_owner, slot_index, column]
    level_mean = mean_counts[classes][..., None, None]
    bias_lin = bias_one[classes][..., None, None]
    bias_sq = bias_two[classes][..., None, None]
    rate_cell = level_mean * jnp.exp(bias_lin * tile_vals + bias_sq * tile_vals * tile_vals)
    score_tile = (cell_counts - rate_cell) * (bias_lin + 2.0 * bias_sq * tile_vals)
    score_field = score_tile.reshape(N_GY, PL, NT, XL, TC).transpose(1, 0, 3, 2, 4).reshape(PL, NG, NG)
    pulled = stencil_sum(score_field, stencil, -1)
    adjoints = [pulled * (1.0 + 2.0 * GROWTH * linear), -pulled * slope_x, -pulled * slope_y, -pulled * shift_x, -pulled * shift_y]
    summed = jnp.fft.fft2(adjoints[0], axes=(1, 2))
    for field_index in range(1, 5):
        summed = summed - 1j * factors[field_index] * jnp.fft.fft2(adjoints[field_index], axes=(1, 2))
    pulled_back = jnp.real(jnp.fft.ifft2(envelope * summed, axes=(1, 2))).astype(jnp.float32)
    return (pulled_back - noise, density)
```

```python
import functools
import math

import jax
import jax.numpy as jnp
import ml_dtypes
import numpy as np
from jax import lax
from jax.experimental import pallas as pl
from jax.experimental.pallas import tpu as pltpu
from jax.sharding import PartitionSpec as P

TC = 128
AMPLITUDE = 0.75
PIVOT = 1.0
GROWTH = 7.0 / 8.0
PAD = 16
VMEM = pltpu.VMEM
F32 = jnp.float32
BF16 = jnp.bfloat16


def split_np(table):
    high = table.astype(np.float32).astype(ml_dtypes.bfloat16)
    low = (table - high.astype(np.float64)).astype(np.float32).astype(ml_dtypes.bfloat16)
    return high, low


def make_tables(side, rows):
    half = side // 2
    quarter = side // 4
    freqs = np.concatenate([np.arange(0, half, 2), np.arange(1, half, 2)])
    wave = 2.0 * math.pi / side * freqs

    def basis(cells):
        turn = (freqs[:, None] * cells[None, :]) % side
        angle = 2.0 * math.pi / side * turn
        cos, sin = np.cos(angle), np.sin(angle)
        return np.concatenate([cos[:quarter], sin[:quarter], cos[quarter:], sin[quarter:]])

    def slope(cells):
        turn = (freqs[:, None] * cells[None, :]) % side
        angle = 2.0 * math.pi / side * turn
        cos, sin = -wave[:, None] * np.sin(angle), wave[:, None] * np.cos(angle)
        return np.concatenate([cos[:quarter], sin[:quarter], cos[quarter:], sin[quarter:]])

    plain = basis(np.arange(half))
    even, odd = plain[:half], plain[half:]
    ring = np.concatenate([np.arange(rows + 1), np.zeros(PAD - 2, int), [side - 1]])
    used = np.ones(rows + PAD)
    used[rows + 1 : rows + PAD - 1] = 0.0
    views = np.concatenate([(basis(ring) * used).T, (slope(ring) * used).T])
    wave_sq = wave[:, None] ** 2 + wave[None, :] ** 2
    inverse = np.where(wave_sq > 0, 1.0 / np.where(wave_sq > 0, wave_sq, 1.0), 0.0)
    weight = np.where(freqs == 0, 1.0, 2.0)
    gain = AMPLITUDE * (np.sqrt(wave_sq) / PIVOT) / (1.0 + wave_sq / PIVOT**2)
    gain = gain * weight[:, None] * weight[None, :] / (side * side)
    views_h, views_l = split_np(views)
    up = views.T
    up_h, up_l = split_np(up)
    tables = []
    for table in (even, odd, even.T, odd.T):
        tables.extend(split_np(np.ascontiguousarray(table)))
    fwd = tuple(tables[:4])
    back = tuple(tables[4:])
    waves = np.repeat(wave.reshape(2, quarter).astype(np.float32)[:, None, :], 1, axis=1)
    return dict(
        fwd=fwd,
        back=back,
        views=(views_h, views_l),
        lift=np.concatenate([up_h, up_h, up_l], axis=1),
        gain=gain.astype(np.float32),
        inverse=inverse.astype(np.float32),
        waves=waves,
    )


def mm(a, b):
    return jnp.dot(a, b, preferred_element_type=F32)


def split(a):
    high = a.astype(BF16)
    return high, (a - high.astype(F32)).astype(BF16)


def mm3(a, b):
    return mm(a[0], b[0]) + (mm(a[0], b[1]) + mm(a[1], b[0]))


def turn_rows(a, step):
    return pltpu.roll(a, step % a.shape[0], 0)


def turn_lanes(a, step):
    return pltpu.roll(a, step % a.shape[1], 1)


def slope_lanes(a, waves, orient):
    q = a.shape[1] // 4
    parts = []
    for par in range(2):
        w = waves[par] * orient
        cos, sin = a[:, 2 * par * q : (2 * par + 1) * q], a[:, (2 * par + 1) * q : (2 * par + 2) * q]
        parts.extend([w * sin, -w * cos])
    return jnp.concatenate(parts, axis=1)


def place_of(me, k, n):
    return lax.rem(lax.bitwise_xor(me, k) - me + n, n)


def main_kernel(n, groups, rows, side, tiles, *refs):
    half, q = side // 2, side // 4
    ring = rows + PAD
    refs = list(refs)
    owner, stencil, mean_counts, bias_one, bias_two = refs[:5]
    blocks = refs[5 : 5 + n]
    msgs = refs[5 + n : 5 + n + groups]
    rest = refs[5 + n + groups :]
    eh, el, oh, ol, teh, tel, toh, tol, vh, vl, lift, gain, inverse, waves = rest[:14]
    density_out = rest[14]
    outs = rest[15 : 15 + n]
    fh, fl, yh, yl, zh, zl, cnt, cls, part = rest[15 + n :]
    me = lax.axis_index("gy")
    mine = lax.axis_index("gx")
    fwd = ((eh, el), (oh, ol))
    back = ((teh, tel), (toh, tol))

    for t in range(tiles):
        rank = jnp.int32(0)
        for t2 in range(t):
            rank = rank + (owner[t2] == owner[t]).astype(jnp.int32)
        which = lax.bitwise_xor(owner[t], mine)
        for k in range(groups):

            @pl.when(which == k)
            def _():
                cnt[:, t * TC : (t + 1) * TC] = msgs[k][rank, :rows, :].astype(F32)
                cls[:, t * TC : (t + 1) * TC] = msgs[k][rank, rows : rows + 8, :]

    for k in range(n // 2):
        a, b = blocks[k][...], blocks[k ^ (n // 2)][...]
        place = place_of(me, k, n)
        sign = jnp.where(place < n // 2, 1.0, -1.0).astype(F32)
        off = pl.multiple_of(lax.rem(place, n // 2) * rows, rows)
        for par, v in ((0, a + b), (1, (a - b) * sign)):
            lo, hi = v[:, :half], v[:, half:]
            for ypar, w in ((0, lo + hi), (1, lo - hi)):
                h, l = split(w)
                fh[par, pl.ds(off, rows), ypar * half : (ypar + 1) * half] = h
                fl[par, pl.ds(off, rows), ypar * half : (ypar + 1) * half] = l

    for par in range(2):
        for ypar in range(2):
            cols = slice(ypar * half, (ypar + 1) * half)
            y = mm3((fh[par, :, cols], fl[par, :, cols]), tuple(r[...] for r in back[ypar]))
            yh[par, :, cols], yl[par, :, cols] = split(y)
    for par in range(2):
        for ypar in range(2):
            cols = slice(ypar * half, (ypar + 1) * half)
            x = mm3(tuple(r[...] for r in fwd[par]), (yh[par, :, cols], yl[par, :, cols]))
            g = gain[par * q : (par + 1) * q, ypar * q : (ypar + 1) * q]
            inv = inverse[par * q : (par + 1) * q, ypar * q : (ypar + 1) * q]
            for i in range(2):
                for j in range(2):
                    base = x[i * q : (i + 1) * q, j * q : (j + 1) * q] * g
                    phi = base * inv
                    rs = slice(par * half + i * q, par * half + (i + 1) * q)
                    c0 = ypar * half + j * q
                    zh[rs, c0 : c0 + q], zl[rs, c0 : c0 + q] = split(base)
                    zh[rs, side + c0 : side + c0 + q], zl[rs, side + c0 : side + c0 + q] = split(phi)

    w = mm3((vh[...], vl[...]), (zh[...], zl[...]))
    ky = (waves[0], waves[1])
    base, base_x = w[:ring, :side], w[ring:, :side]
    phi, phi_x = w[:ring, side:], w[ring:, side:]
    stack = jnp.concatenate([base, phi_x, slope_lanes(phi, ky, 1.0), base_x, slope_lanes(base, ky, 1.0)], axis=0)
    sh, sl = split(stack)
    e = mm3((sh[:, :half], sl[:, :half]), (eh[...], el[...]))
    o = mm3((sh[:, half:], sl[:, half:]), (oh[...], ol[...]))
    fields = jnp.concatenate([e + o, e - o], axis=1)
    linear, shift_x, shift_y, slope_x, slope_y = [fields[i * ring : (i + 1) * ring] for i in range(5)]
    density = linear + GROWTH * linear * linear - (shift_x * slope_x + shift_y * slope_y)
    density_out[...] = density[:rows]

    beside = {0: density, 1: turn_lanes(density, -1), -1: turn_lanes(density, 1)}
    smooth = jnp.zeros_like(density)
    for a in (-1, 0, 1):
        band = sum(stencil[(a + 1) * 3 + b + 1] * beside[b] for b in (-1, 0, 1))
        smooth = smooth + (turn_rows(band, -a) if a else band)
    smooth = smooth[:rows]
    classes = cls[...]
    mean_v, one_v, two_v = [jnp.full(classes.shape, ref[0], F32) for ref in (mean_counts, bias_one, bias_two)]
    for d in range(1, mean_counts.shape[0]):
        hit = classes == d
        mean_v = jnp.where(hit, mean_counts[d], mean_v)
        one_v = jnp.where(hit, bias_one[d], one_v)
        two_v = jnp.where(hit, bias_two[d], two_v)
    mean_v, one_v, two_v = mean_v[:1], one_v[:1], two_v[:1]
    rate = mean_v * jnp.exp(one_v * smooth + two_v * smooth * smooth)
    score = (cnt[...] - rate) * (one_v + 2.0 * two_v * smooth)
    score = jnp.concatenate([score, jnp.zeros((PAD, side), F32)], axis=0)
    beside = {0: score, 1: turn_lanes(score, 1), -1: turn_lanes(score, -1)}
    pulled = jnp.zeros_like(score)
    for a in (-1, 0, 1):
        band = sum(stencil[(a + 1) * 3 + b + 1] * beside[b] for b in (-1, 0, 1))
        pulled = pulled + (turn_rows(band, a) if a else band)

    bars = jnp.concatenate(
        [
            pulled * (1.0 + 2.0 * GROWTH * linear),
            -pulled * slope_x,
            -pulled * slope_y,
            -pulled * shift_x,
            -pulled * shift_y,
        ],
        axis=0,
    )
    lo, hi = bars[:, :half], bars[:, half:]
    ye = mm3(split(lo + hi), (teh[...], tel[...]))
    yo = mm3(split(lo - hi), (toh[...], tol[...]))
    modes = jnp.concatenate([ye, yo], axis=1)
    m_lin, m_sx, m_sy, m_gx, m_gy = [modes[i * ring : (i + 1) * ring] for i in range(5)]
    to_base = m_lin + slope_lanes(m_gy, ky, -1.0)
    to_phi = slope_lanes(m_sy, ky, -1.0)
    pile = jnp.concatenate(
        [jnp.concatenate([to_base, to_phi], axis=1), jnp.concatenate([m_gx, m_sx], axis=1)], axis=0
    )
    ph, plow = split(pile)
    zeros = jnp.zeros((lift.shape[1] - 3 * 2 * ring, 2 * side), BF16)
    pile3 = jnp.concatenate([ph, plow, ph] + ([zeros] if zeros.shape[0] else []), axis=0)

    for par in range(2):
        for i in range(2):
            rs = slice(par * half + i * q, par * half + (i + 1) * q)
            x = mm(lift[rs, :], pile3)
            for ypar in range(2):
                g = gain[par * q : (par + 1) * q, ypar * q : (ypar + 1) * q]
                inv = inverse[par * q : (par + 1) * q, ypar * q : (ypar + 1) * q]
                for j in range(2):
                    c0 = ypar * half + j * q
                    d = g * (x[:, c0 : c0 + q] + inv * x[:, side + c0 : side + c0 + q])
                    yh[par, i * q : (i + 1) * q, c0 : c0 + q], yl[par, i * q : (i + 1) * q, c0 : c0 + q] = split(d)
    e = mm3((teh[...], tel[...]), (yh[0], yl[0]))
    o = mm3((toh[...], tol[...]), (yh[1], yl[1]))
    part[0] = e + o
    part[1] = e - o
    for k in range(n):
        place = place_of(me, k, n)
        off = pl.multiple_of(lax.rem(place, n // 2) * rows, rows)
        outs[k][...] = part[place // (n // 2), pl.ds(off, rows), :]


def last_kernel(count, *refs):
    parts = refs[:count]
    noise, eh, el, oh, ol, out = refs[count:]
    total = parts[0][...]
    for p in parts[1:]:
        total = total + p[...]
    half = total.shape[1] // 2
    sh, sl = split(total)
    e = mm3((sh[:, :half], sl[:, :half]), (eh[...], el[...]))
    o = mm3((sh[:, half:], sl[:, half:]), (oh[...], ol[...]))
    out[:, :half] = e + o - noise[:, :half]
    out[:, half:] = e - o - noise[:, half:]


def local(n, groups, noise, stencil, mean_counts, bias_one, bias_two, owner, depth, counts):
    _, rows, side = noise.shape
    own = noise.reshape(rows, side)
    tiles = side // TC
    slots = counts.shape[1]
    capacity = slots // groups
    tables = make_tables(side, rows)

    def swap(value, k, axis="gy", size=n):
        return lax.ppermute(value, axis, [(i, i ^ k) for i in range(size)])

    blocks = {0: own}
    for k in range(n - 2, 0, -2):
        blocks[k] = swap(own, k)
    blocks[1] = swap(own, 1)
    mine = lax.axis_index("gx")
    message = jnp.concatenate(
        [
            counts.reshape(slots, rows, TC),
            jnp.broadcast_to(depth.reshape(slots, 1, 1), (slots, 8, TC)),
        ],
        axis=1,
    )
    msgs = []
    for k in range(groups):
        piece = lax.dynamic_slice_in_dim(message, lax.bitwise_xor(mine, k) * capacity, capacity, 0)
        msgs.append(swap(piece, k, "gx", groups) if k else piece)
    for k in range(2, n, 2):
        blocks[k + 1] = swap(blocks[k], 1)

    ring = rows + PAD
    half = side // 2
    smem = pl.BlockSpec(memory_space=pltpu.SMEM)
    vmem = pl.BlockSpec(memory_space=VMEM)
    consts = [
        jnp.asarray(t)
        for t in (
            *tables["fwd"],
            *tables["back"],
            *tables["views"],
            tables["lift"],
            tables["gain"],
            tables["inverse"],
            tables["waves"],
        )
    ]
    cell = jax.ShapeDtypeStruct((rows, side), F32)
    density, *parts = pl.pallas_call(
        functools.partial(main_kernel, n, groups, rows, side, tiles),
        out_shape=[cell] * (1 + n),
        in_specs=[smem] * 5 + [vmem] * (n + groups + len(consts)),
        out_specs=[vmem] * (1 + n),
        scratch_shapes=[
            VMEM((2, half, side), BF16),
            VMEM((2, half, side), BF16),
            VMEM((2, half, side), BF16),
            VMEM((2, half, side), BF16),
            VMEM((side, 2 * side), BF16),
            VMEM((side, 2 * side), BF16),
            VMEM((rows, side), F32),
            VMEM((8, side), jnp.int32),
            VMEM((2, half, side), F32),
        ],
        compiler_params=pltpu.CompilerParams(vmem_limit_bytes=32 * 1024 * 1024),
        name="fields_and_adjoint",
    )(
        owner.reshape(tiles),
        stencil,
        mean_counts,
        bias_one,
        bias_two,
        *[blocks[k] for k in range(n)],
        *msgs,
        *consts,
    )
    sums = {}
    for k in range(n - 2, -1, -2):
        sums[k] = parts[k] + swap(parts[k + 1], 1)
    pieces = [sums[0]] + [swap(sums[k], k) for k in range(n - 2, 0, -2)]
    gradient = pl.pallas_call(
        functools.partial(last_kernel, len(pieces)),
        out_shape=cell,
        in_specs=[vmem] * (len(pieces) + 5),
        out_specs=vmem,
        compiler_params=pltpu.CompilerParams(vmem_limit_bytes=32 * 1024 * 1024),
        name="sum_and_rows",
    )(*pieces, own, *consts[:4])
    return (gradient.reshape(1, rows, side), density.reshape(1, rows, side))


def solution(mesh):
    return jax.shard_map(
        functools.partial(local, mesh.shape["gy"], mesh.shape["gx"]),
        mesh=mesh,
        in_specs=(
            P("gx", "gy", None),
            P(),
            P(),
            P(),
            P(),
            P("gy", "gx", None, None),
            P("gx", None, "gy"),
            P("gx", None, "gy", None, None),
        ),
        out_specs=(P("gx", "gy", None), P("gx", "gy", None)),
        check_vma=False,
    )
```

```python
import functools
import math

import jax
import jax.numpy as jnp
import ml_dtypes
import numpy as np
from jax import lax
from jax.experimental import pallas as pl
from jax.experimental.pallas import tpu as pltpu
from jax.sharding import PartitionSpec as P

TC = 128
AMPLITUDE = 0.75
PIVOT = 1.0
GROWTH = 7.0 / 8.0
PAD = 16
MIB = 1024 * 1024
VMEM = pltpu.VMEM
F32 = jnp.float32
BF16 = jnp.bfloat16


def split_np(table):
    high = table.astype(np.float32).astype(ml_dtypes.bfloat16)
    low = (table - high.astype(np.float64)).astype(np.float32).astype(ml_dtypes.bfloat16)
    return high, low


def make_tables(side, rows):
    half = side // 2
    quarter = side // 4
    freqs = np.concatenate([np.arange(0, half, 2), np.arange(1, half, 2)])
    wave = 2.0 * math.pi / side * freqs

    def basis(cells):
        turn = (freqs[:, None] * cells[None, :]) % side
        angle = 2.0 * math.pi / side * turn
        cos, sin = np.cos(angle), np.sin(angle)
        return np.concatenate([cos[:quarter], sin[:quarter], cos[quarter:], sin[quarter:]])

    def slope(cells):
        turn = (freqs[:, None] * cells[None, :]) % side
        angle = 2.0 * math.pi / side * turn
        cos, sin = -wave[:, None] * np.sin(angle), wave[:, None] * np.cos(angle)
        return np.concatenate([cos[:quarter], sin[:quarter], cos[quarter:], sin[quarter:]])

    plain = basis(np.arange(half))
    even, odd = plain[:half], plain[half:]
    ring = np.concatenate([np.arange(rows + 1), np.zeros(PAD - 2, int), [side - 1]])
    used = np.ones(rows + PAD)
    used[rows + 1 : rows + PAD - 1] = 0.0
    views = np.concatenate([(basis(ring) * used).T, (slope(ring) * used).T])
    wave_sq = wave[:, None] ** 2 + wave[None, :] ** 2
    inverse = np.where(wave_sq > 0, 1.0 / np.where(wave_sq > 0, wave_sq, 1.0), 0.0)
    weight = np.where(freqs == 0, 1.0, 2.0)
    gain = AMPLITUDE * (np.sqrt(wave_sq) / PIVOT) / (1.0 + wave_sq / PIVOT**2)
    gain = gain * weight[:, None] * weight[None, :] / (side * side)
    sections = []
    for table in (even, odd, even.T, odd.T):
        sections.append(np.concatenate(split_np(np.ascontiguousarray(table)), axis=1))
    sections.extend(split_np(views))
    up_h, up_l = split_np(np.ascontiguousarray(views.T))
    lift = np.concatenate([up_h, up_h, up_l], axis=1)
    sections.append(np.concatenate([lift, np.zeros((side, side - lift.shape[1]), lift.dtype)], axis=1))
    waves = np.zeros((8, half))
    waves[:] = wave[None, :]
    return np.concatenate(sections), np.concatenate([gain, inverse, waves]).astype(np.float32)


class Tables:
    def __init__(self, packed, reals, side, ring):
        half = side // 2
        self.half = half
        self.ring = ring
        self.packed = packed
        self.reals = reals
        self.lift_at = 4 * half + 4 * ring

    def _pair(self, at):
        half = self.half
        return self.packed[at : at + half, :half], self.packed[at : at + half, half:]

    def fwd(self, par):
        return self._pair(par * self.half)

    def back(self, par):
        return self._pair((2 + par) * self.half)

    def views(self):
        at, count = 4 * self.half, 2 * self.ring
        return self.packed[at : at + count, :], self.packed[at + count : at + 2 * count, :]

    def lift(self, start, count):
        return self.packed[self.lift_at + start : self.lift_at + start + count, : 6 * self.ring]

    def gain(self, par, ypar):
        q = self.half // 2
        return self.reals[par * q : (par + 1) * q, ypar * q : (ypar + 1) * q]

    def inverse(self, par, ypar):
        q, half = self.half // 2, self.half
        return self.reals[half + par * q : half + (par + 1) * q, ypar * q : (ypar + 1) * q]

    def waves(self):
        q, half = self.half // 2, self.half
        row = self.reals[2 * half : 2 * half + 1, :]
        return row[:, :q], row[:, q:]


def mm(a, b):
    return jnp.dot(a, b, preferred_element_type=F32)


def split(a):
    high = a.astype(BF16)
    return high, (a - high.astype(F32)).astype(BF16)


def mm3(a, b):
    return mm(a[0], b[0]) + (mm(a[0], b[1]) + mm(a[1], b[0]))


def turn_rows(a, step):
    return pltpu.roll(a, step % a.shape[0], 0)


def turn_lanes(a, step):
    return pltpu.roll(a, step % a.shape[1], 1)


def slope_lanes(a, waves, orient):
    q = a.shape[1] // 4
    parts = []
    for par in range(2):
        w = waves[par] * orient
        cos, sin = a[:, 2 * par * q : (2 * par + 1) * q], a[:, (2 * par + 1) * q : (2 * par + 2) * q]
        parts.extend([w * sin, -w * cos])
    return jnp.concatenate(parts, axis=1)


def place_of(me, k, n):
    return lax.rem(lax.bitwise_xor(me, k) - me + n, n)


def main_kernel(n, groups, rows, side, tiles, *refs):
    half, q = side // 2, side // 4
    ring = rows + PAD
    refs = list(refs)
    small = refs[:5]
    blocks = refs[5 : 5 + n]
    msgs = refs[5 + n : 5 + n + groups]
    rest = refs[5 + n + groups :]
    tabs = Tables(rest[0], rest[1], side, ring)
    density_out = rest[2]
    outs = rest[3 : 3 + n]
    fh, fl, yh, yl, zh, zl, cnt, cls, part = rest[3 + n : 12 + n]
    held = rest[12 + n : 17 + n]
    sems = rest[17 + n]
    owner, stencil, mean_counts, bias_one, bias_two = held
    copies = [pltpu.make_async_copy(a, b, sems.at[i]) for i, (a, b) in enumerate(zip(small, held))]
    for copy in copies:
        copy.start()
    me = lax.axis_index("gy")
    mine = lax.axis_index("gx")

    for k in range(n // 2):
        a, b = blocks[k][...], blocks[k ^ (n // 2)][...]
        place = place_of(me, k, n)
        sign = jnp.where(place < n // 2, 1.0, -1.0).astype(F32)
        off = pl.multiple_of(lax.rem(place, n // 2) * rows, rows)
        for par, v in ((0, a + b), (1, (a - b) * sign)):
            lo, hi = v[:, :half], v[:, half:]
            for ypar, w in ((0, lo + hi), (1, lo - hi)):
                h, l = split(w)
                fh[par, pl.ds(off, rows), ypar * half : (ypar + 1) * half] = h
                fl[par, pl.ds(off, rows), ypar * half : (ypar + 1) * half] = l

    for par in range(2):
        for ypar in range(2):
            cols = slice(ypar * half, (ypar + 1) * half)
            y = mm3((fh[par, :, cols], fl[par, :, cols]), tabs.back(ypar))
            yh[par, :, cols], yl[par, :, cols] = split(y)
    for par in range(2):
        for ypar in range(2):
            cols = slice(ypar * half, (ypar + 1) * half)
            x = mm3(tabs.fwd(par), (yh[par, :, cols], yl[par, :, cols]))
            g = tabs.gain(par, ypar)
            inv = tabs.inverse(par, ypar)
            for i in range(2):
                for j in range(2):
                    base = x[i * q : (i + 1) * q, j * q : (j + 1) * q] * g
                    phi = base * inv
                    rs = slice(par * half + i * q, par * half + (i + 1) * q)
                    c0 = ypar * half + j * q
                    zh[rs, c0 : c0 + q], zl[rs, c0 : c0 + q] = split(base)
                    zh[rs, side + c0 : side + c0 + q], zl[rs, side + c0 : side + c0 + q] = split(phi)

    w = mm3(tabs.views(), (zh[...], zl[...]))
    ky = tabs.waves()
    base, base_x = w[:ring, :side], w[ring:, :side]
    phi, phi_x = w[:ring, side:], w[ring:, side:]
    stack = jnp.concatenate([base, phi_x, slope_lanes(phi, ky, 1.0), base_x, slope_lanes(base, ky, 1.0)], axis=0)
    sh, sl = split(stack)
    e = mm3((sh[:, :half], sl[:, :half]), tabs.fwd(0))
    o = mm3((sh[:, half:], sl[:, half:]), tabs.fwd(1))
    fields = jnp.concatenate([e + o, e - o], axis=1)
    linear, shift_x, shift_y, slope_x, slope_y = [fields[i * ring : (i + 1) * ring] for i in range(5)]
    density = linear + GROWTH * linear * linear - (shift_x * slope_x + shift_y * slope_y)
    density_out[...] = density[:rows]

    for copy in copies:
        copy.wait()

    for t in range(tiles):
        rank = jnp.int32(0)
        for t2 in range(t):
            rank = rank + (owner[t2] == owner[t]).astype(jnp.int32)
        which = lax.bitwise_xor(owner[t], mine)
        for k in range(groups):

            @pl.when(which == k)
            def _():
                cnt[:, t * TC : (t + 1) * TC] = msgs[k][rank, :rows, :].astype(F32)
                cls[:, t * TC : (t + 1) * TC] = msgs[k][rank, rows : rows + 8, :]

    beside = {0: density, 1: turn_lanes(density, -1), -1: turn_lanes(density, 1)}
    smooth = jnp.zeros_like(density)
    for a in (-1, 0, 1):
        band = sum(stencil[(a + 1) * 3 + b + 1] * beside[b] for b in (-1, 0, 1))
        smooth = smooth + (turn_rows(band, -a) if a else band)
    smooth = smooth[:rows]
    classes = cls[...]
    mean_v, one_v, two_v = [jnp.full(classes.shape, ref[0], F32) for ref in (mean_counts, bias_one, bias_two)]
    for d in range(1, mean_counts.shape[0]):
        hit = classes == d
        mean_v = jnp.where(hit, mean_counts[d], mean_v)
        one_v = jnp.where(hit, bias_one[d], one_v)
        two_v = jnp.where(hit, bias_two[d], two_v)
    mean_v, one_v, two_v = mean_v[:1], one_v[:1], two_v[:1]
    rate = mean_v * jnp.exp(one_v * smooth + two_v * smooth * smooth)
    score = (cnt[...] - rate) * (one_v + 2.0 * two_v * smooth)
    score = jnp.concatenate([score, jnp.zeros((PAD, side), F32)], axis=0)
    beside = {0: score, 1: turn_lanes(score, 1), -1: turn_lanes(score, -1)}
    pulled = jnp.zeros_like(score)
    for a in (-1, 0, 1):
        band = sum(stencil[(a + 1) * 3 + b + 1] * beside[b] for b in (-1, 0, 1))
        pulled = pulled + (turn_rows(band, a) if a else band)

    bars = jnp.concatenate(
        [
            pulled * (1.0 + 2.0 * GROWTH * linear),
            -pulled * slope_x,
            -pulled * slope_y,
            -pulled * shift_x,
            -pulled * shift_y,
        ],
        axis=0,
    )
    lo, hi = bars[:, :half], bars[:, half:]
    ye = mm3(split(lo + hi), tabs.back(0))
    yo = mm3(split(lo - hi), tabs.back(1))
    modes = jnp.concatenate([ye, yo], axis=1)
    m_lin, m_sx, m_sy, m_gx, m_gy = [modes[i * ring : (i + 1) * ring] for i in range(5)]
    to_base = m_lin + slope_lanes(m_gy, ky, -1.0)
    to_phi = slope_lanes(m_sy, ky, -1.0)
    pile = jnp.concatenate(
        [jnp.concatenate([to_base, to_phi], axis=1), jnp.concatenate([m_gx, m_sx], axis=1)], axis=0
    )
    ph, plow = split(pile)
    pile3 = jnp.concatenate([ph, plow, ph], axis=0)

    for par in range(2):
        for i in range(2):
            rs = slice(par * half + i * q, par * half + (i + 1) * q)
            x = mm(tabs.lift(rs.start, q), pile3)
            for ypar in range(2):
                g = tabs.gain(par, ypar)
                inv = tabs.inverse(par, ypar)
                for j in range(2):
                    c0 = ypar * half + j * q
                    d = g * (x[:, c0 : c0 + q] + inv * x[:, side + c0 : side + c0 + q])
                    yh[par, i * q : (i + 1) * q, c0 : c0 + q], yl[par, i * q : (i + 1) * q, c0 : c0 + q] = split(d)
    e = mm3(tabs.back(0), (yh[0], yl[0]))
    o = mm3(tabs.back(1), (yh[1], yl[1]))
    part[0] = e + o
    part[1] = e - o
    for k in range(n):
        place = place_of(me, k, n)
        off = pl.multiple_of(lax.rem(place, n // 2) * rows, rows)
        outs[k][...] = part[place // (n // 2), pl.ds(off, rows), :]


def message_kernel(groups, capacity, rows, counts, depth, noise, *refs):
    msgs = refs[:groups]
    noise_out, classes, sems = refs[groups:]
    mine = lax.axis_index("gx")
    first = pltpu.make_async_copy(depth, classes, sems.at[groups])
    first.start()
    copies = []
    for k in range(groups):
        start = lax.bitwise_xor(mine, k) * capacity
        copies.append(
            pltpu.make_async_copy(
                counts.at[pl.ds(start, capacity)], msgs[k].at[:, pl.ds(0, rows), :], sems.at[k]
            )
        )
        copies[k].start()
    copies.append(pltpu.make_async_copy(noise, noise_out, sems.at[groups + 1]))
    copies[groups].start()
    first.wait()
    for k in range(groups):
        start = lax.bitwise_xor(mine, k) * capacity
        for r in range(capacity):
            msgs[k][r, rows : rows + 8, :] = jnp.full((8, TC), classes[start + r], jnp.int32)
    for copy in copies:
        copy.wait()


def table_kernel(packed, reals, packed_out, reals_out, sems):
    copies = [
        pltpu.make_async_copy(packed, packed_out, sems.at[0]),
        pltpu.make_async_copy(reals, reals_out, sems.at[1]),
    ]
    for copy in copies:
        copy.start()
    for copy in copies:
        copy.wait()


def in_hbm(value):
    return pltpu.with_memory_space_constraint(value, pltpu.HBM)


def last_kernel(count, *refs):
    parts = refs[:count]
    noise, packed, out = refs[count:]
    total = parts[0][...]
    for p in parts[1:]:
        total = total + p[...]
    half = total.shape[1] // 2
    tabs = Tables(packed, None, 2 * half, 0)
    sh, sl = split(total)
    e = mm3((sh[:, :half], sl[:, :half]), tabs.fwd(0))
    o = mm3((sh[:, half:], sl[:, half:]), tabs.fwd(1))
    out[:, :half] = e + o - noise[:, :half]
    out[:, half:] = e - o - noise[:, half:]


def local(n, groups, noise, stencil, mean_counts, bias_one, bias_two, owner, depth, counts):
    _, rows, side = noise.shape
    own = noise.reshape(rows, side)
    tiles = side // TC
    slots = counts.shape[1]
    capacity = slots // groups
    packed, reals = [jnp.asarray(t) for t in make_tables(side, rows)]
    vmem = pl.BlockSpec(memory_space=VMEM)
    hbm = pl.BlockSpec(memory_space=pltpu.HBM)

    def swap(value, k, axis="gy", size=n):
        return lax.ppermute(value, axis, [(i, i ^ k) for i in range(size)])

    blocks = {}
    for k in range(n - 2, 0, -2):
        blocks[k] = swap(own, k)
    *msgs, held_own = pl.pallas_call(
        functools.partial(message_kernel, groups, capacity, rows),
        out_shape=[VMEM((capacity, rows + 8, TC), jnp.int32)] * groups + [VMEM((rows, side), F32)],
        in_specs=[hbm] * 3,
        out_specs=[vmem] * (groups + 1),
        scratch_shapes=[pltpu.SMEM((slots,), jnp.int32), pltpu.SemaphoreType.DMA((groups + 2,))],
        compiler_params=pltpu.CompilerParams(vmem_limit_bytes=4 * MIB),
        name="messages",
    )(in_hbm(counts.reshape(slots, rows, TC)), in_hbm(depth.reshape(slots)), in_hbm(own))
    for k in range(groups - 1, 0, -1):
        if k == 1:
            msgs[k], _ = lax.optimization_barrier((msgs[k], blocks[n - 2]))
        msgs[k] = swap(msgs[k], k, "gx", groups)
    blocks[0], _ = lax.optimization_barrier((held_own, blocks[n - 2]))
    blocks[1] = swap(blocks[0], 1)
    for k in range(n - 2, 0, -2):
        blocks[k + 1] = swap(blocks[k], 1)
    packed, reals, _ = lax.optimization_barrier((packed, reals, blocks[n - 2]))
    packed, reals = pl.pallas_call(
        table_kernel,
        out_shape=[VMEM(t.shape, t.dtype) for t in (packed, reals)],
        in_specs=[hbm] * 2,
        out_specs=[vmem] * 2,
        scratch_shapes=[pltpu.SemaphoreType.DMA((2,))],
        compiler_params=pltpu.CompilerParams(vmem_limit_bytes=4 * MIB),
        name="tables",
    )(in_hbm(packed), in_hbm(reals))
    half = side // 2
    cell = jax.ShapeDtypeStruct((rows, side), F32)
    small = (owner.reshape(tiles), stencil, mean_counts, bias_one, bias_two)
    density, *parts = pl.pallas_call(
        functools.partial(main_kernel, n, groups, rows, side, tiles),
        out_shape=[cell] * (1 + n),
        in_specs=[hbm] * 5 + [vmem] * (n + groups + 2),
        out_specs=[vmem] * (1 + n),
        scratch_shapes=[
            VMEM((2, half, side), BF16),
            VMEM((2, half, side), BF16),
            VMEM((2, half, side), BF16),
            VMEM((2, half, side), BF16),
            VMEM((side, 2 * side), BF16),
            VMEM((side, 2 * side), BF16),
            VMEM((rows, side), F32),
            VMEM((8, side), jnp.int32),
            VMEM((2, half, side), F32),
            *[pltpu.SMEM(a.shape, a.dtype) for a in small],
            pltpu.SemaphoreType.DMA((5,)),
        ],
        compiler_params=pltpu.CompilerParams(vmem_limit_bytes=16 * MIB),
        name="fields_and_adjoint",
    )(
        *[in_hbm(a) for a in small],
        *[blocks[k] for k in range(n)],
        *msgs,
        packed,
        reals,
    )
    sums = {}
    for k in range(n - 2, -1, -2):
        sums[k] = parts[k] + swap(parts[k + 1], 1)
    pieces = [sums[0]] + [swap(sums[k], k) for k in range(n - 2, 0, -2)]
    gradient = pl.pallas_call(
        functools.partial(last_kernel, len(pieces)),
        out_shape=cell,
        in_specs=[vmem] * (len(pieces) + 2),
        out_specs=vmem,
        compiler_params=pltpu.CompilerParams(vmem_limit_bytes=8 * MIB),
        name="sum_and_rows",
    )(*pieces, blocks[0], packed)
    return (gradient.reshape(1, rows, side), density.reshape(1, rows, side))


def solution(mesh):
    return jax.shard_map(
        functools.partial(local, mesh.shape["gy"], mesh.shape["gx"]),
        mesh=mesh,
        in_specs=(
            P("gx", "gy", None),
            P(),
            P(),
            P(),
            P(),
            P("gy", "gx", None, None),
            P("gx", None, "gy"),
            P("gx", None, "gy", None, None),
        ),
        out_specs=(P("gx", "gy", None), P("gx", "gy", None)),
        check_vma=False,
    )
```

```python
import functools
import math

import jax
import jax.numpy as jnp
import ml_dtypes
import numpy as np
from jax import lax
from jax.experimental import pallas as pl
from jax.experimental.pallas import tpu as pltpu
from jax.sharding import PartitionSpec as P

TC = 128
AMPLITUDE = 0.75
PIVOT = 1.0
GROWTH = 7.0 / 8.0
PAD = 16
MIB = 1024 * 1024
VMEM = pltpu.VMEM
F32 = jnp.float32
BF16 = jnp.bfloat16


def split_np(table):
    high = table.astype(np.float32).astype(ml_dtypes.bfloat16)
    low = (table - high.astype(np.float64)).astype(np.float32).astype(ml_dtypes.bfloat16)
    return high, low


def make_tables(side, rows):
    half = side // 2
    quarter = side // 4
    freqs = np.concatenate([np.arange(0, half, 2), np.arange(1, half, 2)])
    wave = 2.0 * math.pi / side * freqs

    def basis(cells):
        turn = (freqs[:, None] * cells[None, :]) % side
        angle = 2.0 * math.pi / side * turn
        cos, sin = np.cos(angle), np.sin(angle)
        return np.concatenate([cos[:quarter], sin[:quarter], cos[quarter:], sin[quarter:]])

    def slope(cells):
        turn = (freqs[:, None] * cells[None, :]) % side
        angle = 2.0 * math.pi / side * turn
        cos, sin = -wave[:, None] * np.sin(angle), wave[:, None] * np.cos(angle)
        return np.concatenate([cos[:quarter], sin[:quarter], cos[quarter:], sin[quarter:]])

    plain = basis(np.arange(half))
    even, odd = plain[:half], plain[half:]
    ring = np.concatenate([np.arange(rows + 1), np.zeros(PAD - 2, int), [side - 1]])
    used = np.ones(rows + PAD)
    used[rows + 1 : rows + PAD - 1] = 0.0
    views = np.concatenate([(basis(ring) * used).T, (slope(ring) * used).T])
    wave_sq = wave[:, None] ** 2 + wave[None, :] ** 2
    inverse = np.where(wave_sq > 0, 1.0 / np.where(wave_sq > 0, wave_sq, 1.0), 0.0)
    weight = np.where(freqs == 0, 1.0, 2.0)
    gain = AMPLITUDE * (np.sqrt(wave_sq) / PIVOT) / (1.0 + wave_sq / PIVOT**2)
    gain = gain * weight[:, None] * weight[None, :] / (side * side)
    sections = []
    for table in (even, odd, even.T, odd.T):
        sections.append(np.concatenate(split_np(np.ascontiguousarray(table)), axis=1))
    sections.extend(split_np(views))
    up_h, up_l = split_np(np.ascontiguousarray(views.T))
    lift = np.concatenate([up_h, up_h, up_l], axis=1)
    sections.append(np.concatenate([lift, np.zeros((side, side - lift.shape[1]), lift.dtype)], axis=1))
    waves = np.zeros((8, half))
    waves[:] = wave[None, :]
    return (
        np.concatenate(sections[2:4]),
        np.concatenate(sections[:2] + sections[4:]),
        np.concatenate([gain, inverse, waves]).astype(np.float32),
    )


class Tables:
    def __init__(self, backs, packed, reals, side, ring):
        half = side // 2
        self.half = half
        self.ring = ring
        self.backs = backs
        self.packed = packed
        self.reals = reals
        self.lift_at = 2 * half + 4 * ring

    def fwd(self, par):
        half, at = self.half, par * self.half
        return self.packed[at : at + half, :half], self.packed[at : at + half, half:]

    def back(self, par):
        half, at = self.half, par * self.half
        return self.backs[at : at + half, :half], self.backs[at : at + half, half:]

    def views(self):
        at, count = 2 * self.half, 2 * self.ring
        return self.packed[at : at + count, :], self.packed[at + count : at + 2 * count, :]

    def lift(self, start, count):
        return self.packed[self.lift_at + start : self.lift_at + start + count, : 6 * self.ring]

    def gain(self, par, ypar):
        q = self.half // 2
        return self.reals[par * q : (par + 1) * q, ypar * q : (ypar + 1) * q]

    def inverse(self, par, ypar):
        q, half = self.half // 2, self.half
        return self.reals[half + par * q : half + (par + 1) * q, ypar * q : (ypar + 1) * q]

    def waves(self):
        q, half = self.half // 2, self.half
        row = self.reals[2 * half : 2 * half + 1, :]
        return row[:, :q], row[:, q:]


def mm(a, b):
    return jnp.dot(a, b, preferred_element_type=F32)


def split(a):
    high = a.astype(BF16)
    return high, (a - high.astype(F32)).astype(BF16)


def mm3(a, b):
    return mm(a[0], b[0]) + (mm(a[0], b[1]) + mm(a[1], b[0]))


def turn_rows(a, step):
    return pltpu.roll(a, step % a.shape[0], 0)


def turn_lanes(a, step):
    return pltpu.roll(a, step % a.shape[1], 1)


def slope_lanes(a, waves, orient):
    q = a.shape[1] // 4
    parts = []
    for par in range(2):
        w = waves[par] * orient
        cos, sin = a[:, 2 * par * q : (2 * par + 1) * q], a[:, (2 * par + 1) * q : (2 * par + 2) * q]
        parts.extend([w * sin, -w * cos])
    return jnp.concatenate(parts, axis=1)


def place_of(me, k, n):
    return lax.rem(lax.bitwise_xor(me, k) - me + n, n)


def along_y_kernel(n, rows, side, *refs):
    half = side // 2
    blocks = refs[: n // 2]
    backs, out, fh, fl = refs[n // 2 :]
    tabs = Tables(backs, None, None, side, 0)
    me = lax.axis_index("gy")
    for i in range(n // 4):
        a, b = blocks[i][...], blocks[i + n // 4][...]
        place = place_of(me, 2 * i, n)
        sign = jnp.where(place < n // 2, 1.0, -1.0).astype(F32)
        off = pl.multiple_of(lax.rem(place, n // 2) // 2 * rows, rows)
        for par, v in ((0, a + b), (1, (a - b) * sign)):
            lo, hi = v[:, :half], v[:, half:]
            for ypar, w in ((0, lo + hi), (1, lo - hi)):
                h, l = split(w)
                fh[par, pl.ds(off, rows), ypar * half : (ypar + 1) * half] = h
                fl[par, pl.ds(off, rows), ypar * half : (ypar + 1) * half] = l
    for par in range(2):
        for ypar in range(2):
            cols = slice(ypar * half, (ypar + 1) * half)
            out[par, :, cols] = mm3((fh[par, :, cols], fl[par, :, cols]), tabs.back(ypar))


def field_kernel(n, rows, side, *refs):
    half, q = side // 2, side // 4
    ring = rows + PAD
    stencil_in, own, other, packed, reals = refs[:5]
    density_out, smooth_out, fields_out = refs[5:8]
    yh, yl, zh, zl, stencil, sem = refs[8:]
    tabs = Tables(None, packed, reals, side, ring)
    load = pltpu.make_async_copy(stencil_in, stencil, sem)
    load.start()

    odd = lax.rem(lax.axis_index("gy"), 2)
    for i in range(n // 4):
        place = jnp.where(odd == 1, (2 * i - 1) % (n // 2), 2 * i + 1)
        off = pl.multiple_of(place * rows, rows)
        sign = jnp.where(odd == 1, -1.0, 1.0).astype(F32) if i == 0 else 1.0
        rs = slice(i * rows, (i + 1) * rows)
        for par in range(2):
            yh[par, 2 * i * rows : (2 * i + 1) * rows, :], yl[par, 2 * i * rows : (2 * i + 1) * rows, :] = split(
                own[par, rs, :]
            )
            v = other[par, rs, :]
            h, l = split(v * sign if par else v)
            yh[par, pl.ds(off, rows), :] = h
            yl[par, pl.ds(off, rows), :] = l

    for par in range(2):
        for ypar in range(2):
            cols = slice(ypar * half, (ypar + 1) * half)
            x = mm3(tabs.fwd(par), (yh[par, :, cols], yl[par, :, cols]))
            g = tabs.gain(par, ypar)
            inv = tabs.inverse(par, ypar)
            for i in range(2):
                for j in range(2):
                    base = x[i * q : (i + 1) * q, j * q : (j + 1) * q] * g
                    phi = base * inv
                    rs = slice(par * half + i * q, par * half + (i + 1) * q)
                    c0 = ypar * half + j * q
                    zh[rs, c0 : c0 + q], zl[rs, c0 : c0 + q] = split(base)
                    zh[rs, side + c0 : side + c0 + q], zl[rs, side + c0 : side + c0 + q] = split(phi)

    w = mm3(tabs.views(), (zh[...], zl[...]))
    ky = tabs.waves()
    base, base_x = w[:ring, :side], w[ring:, :side]
    phi, phi_x = w[:ring, side:], w[ring:, side:]
    stack = jnp.concatenate([base, phi_x, slope_lanes(phi, ky, 1.0), base_x, slope_lanes(base, ky, 1.0)], axis=0)
    sh, sl = split(stack)
    e = mm3((sh[:, :half], sl[:, :half]), tabs.fwd(0))
    o = mm3((sh[:, half:], sl[:, half:]), tabs.fwd(1))
    fields = jnp.concatenate([e + o, e - o], axis=1)
    fields_out[...] = fields
    linear, shift_x, shift_y, slope_x, slope_y = [fields[i * ring : (i + 1) * ring] for i in range(5)]
    density = linear + GROWTH * linear * linear - (shift_x * slope_x + shift_y * slope_y)
    density_out[...] = density[:rows]

    load.wait()
    beside = {0: density, 1: turn_lanes(density, -1), -1: turn_lanes(density, 1)}
    smooth = jnp.zeros_like(density)
    for a in (-1, 0, 1):
        band = sum(stencil[(a + 1) * 3 + b + 1] * beside[b] for b in (-1, 0, 1))
        smooth = smooth + (turn_rows(band, -a) if a else band)
    smooth_out[...] = smooth[:rows]


def adjoint_kernel(n, groups, rows, side, tiles, *refs):
    half, q = side // 2, side // 4
    ring = rows + PAD
    small = refs[:5]
    msgs = refs[5 : 5 + groups]
    smooth_in, fields, backs, packed, reals = refs[5 + groups : 10 + groups]
    outs = refs[10 + groups : 10 + groups + n]
    yh, yl, cnt, cls, part, *held, sems = refs[10 + groups + n :]
    owner, stencil, mean_counts, bias_one, bias_two = held
    tabs = Tables(backs, packed, reals, side, ring)
    ky = tabs.waves()
    me = lax.axis_index("gy")
    mine = lax.axis_index("gx")
    copies = [pltpu.make_async_copy(a, b, sems.at[i]) for i, (a, b) in enumerate(zip(small, held))]
    for copy in copies:
        copy.start()
    for copy in copies:
        copy.wait()

    for t in range(tiles):
        rank = jnp.int32(0)
        for t2 in range(t):
            rank = rank + (owner[t2] == owner[t]).astype(jnp.int32)
        which = lax.bitwise_xor(owner[t], mine)
        for k in range(groups):

            @pl.when(which == k)
            def _():
                cnt[:, t * TC : (t + 1) * TC] = msgs[k][rank, :rows, :].astype(F32)
                cls[:, t * TC : (t + 1) * TC] = msgs[k][rank, rows : rows + 8, :]

    smooth = smooth_in[...]
    linear, shift_x, shift_y, slope_x, slope_y = [fields[i * ring : (i + 1) * ring, :] for i in range(5)]
    classes = cls[...]
    mean_v, one_v, two_v = [jnp.full(classes.shape, ref[0], F32) for ref in (mean_counts, bias_one, bias_two)]
    for d in range(1, mean_counts.shape[0]):
        hit = classes == d
        mean_v = jnp.where(hit, mean_counts[d], mean_v)
        one_v = jnp.where(hit, bias_one[d], one_v)
        two_v = jnp.where(hit, bias_two[d], two_v)
    mean_v, one_v, two_v = mean_v[:1], one_v[:1], two_v[:1]
    rate = mean_v * jnp.exp(one_v * smooth + two_v * smooth * smooth)
    score = (cnt[...] - rate) * (one_v + 2.0 * two_v * smooth)
    score = jnp.concatenate([score, jnp.zeros((PAD, side), F32)], axis=0)
    beside = {0: score, 1: turn_lanes(score, 1), -1: turn_lanes(score, -1)}
    pulled = jnp.zeros_like(score)
    for a in (-1, 0, 1):
        band = sum(stencil[(a + 1) * 3 + b + 1] * beside[b] for b in (-1, 0, 1))
        pulled = pulled + (turn_rows(band, a) if a else band)

    bars = jnp.concatenate(
        [
            pulled * (1.0 + 2.0 * GROWTH * linear),
            -pulled * slope_x,
            -pulled * slope_y,
            -pulled * shift_x,
            -pulled * shift_y,
        ],
        axis=0,
    )
    lo, hi = bars[:, :half], bars[:, half:]
    ye = mm3(split(lo + hi), tabs.back(0))
    yo = mm3(split(lo - hi), tabs.back(1))
    modes = jnp.concatenate([ye, yo], axis=1)
    m_lin, m_sx, m_sy, m_gx, m_gy = [modes[i * ring : (i + 1) * ring] for i in range(5)]
    to_base = m_lin + slope_lanes(m_gy, ky, -1.0)
    to_phi = slope_lanes(m_sy, ky, -1.0)
    pile = jnp.concatenate(
        [jnp.concatenate([to_base, to_phi], axis=1), jnp.concatenate([m_gx, m_sx], axis=1)], axis=0
    )
    ph, plow = split(pile)
    pile3 = jnp.concatenate([ph, plow, ph], axis=0)

    for par in range(2):
        for i in range(2):
            rs = slice(par * half + i * q, par * half + (i + 1) * q)
            x = mm(tabs.lift(rs.start, q), pile3)
            for ypar in range(2):
                g = tabs.gain(par, ypar)
                inv = tabs.inverse(par, ypar)
                for j in range(2):
                    c0 = ypar * half + j * q
                    d = g * (x[:, c0 : c0 + q] + inv * x[:, side + c0 : side + c0 + q])
                    yh[par, i * q : (i + 1) * q, c0 : c0 + q], yl[par, i * q : (i + 1) * q, c0 : c0 + q] = split(d)
    e = mm3(tabs.back(0), (yh[0], yl[0]))
    o = mm3(tabs.back(1), (yh[1], yl[1]))
    part[0] = e + o
    part[1] = e - o
    for k in range(n):
        place = place_of(me, k, n)
        off = pl.multiple_of(lax.rem(place, n // 2) * rows, rows)
        outs[k][...] = part[place // (n // 2), pl.ds(off, rows), :]


def message_kernel(groups, capacity, rows, counts, depth, noise, *refs):
    msgs = refs[:groups]
    noise_out, classes, sems = refs[groups:]
    mine = lax.axis_index("gx")
    first = pltpu.make_async_copy(depth, classes, sems.at[groups])
    first.start()
    copies = []
    for k in range(groups):
        start = lax.bitwise_xor(mine, k) * capacity
        copies.append(
            pltpu.make_async_copy(
                counts.at[pl.ds(start, capacity)], msgs[k].at[:, pl.ds(0, rows), :], sems.at[k]
            )
        )
        copies[k].start()
    copies.append(pltpu.make_async_copy(noise, noise_out, sems.at[groups + 1]))
    copies[groups].start()
    first.wait()
    for k in range(groups):
        start = lax.bitwise_xor(mine, k) * capacity
        for r in range(capacity):
            msgs[k][r, rows : rows + 8, :] = jnp.full((8, TC), classes[start + r], jnp.int32)
    for copy in copies:
        copy.wait()


def table_kernel(*refs):
    sems = refs[-1]
    count = len(refs) // 2
    copies = [pltpu.make_async_copy(refs[i], refs[count + i], sems.at[i]) for i in range(count)]
    for copy in copies:
        copy.start()
    for copy in copies:
        copy.wait()


def in_hbm(value):
    return pltpu.with_memory_space_constraint(value, pltpu.HBM)


def last_kernel(count, *refs):
    parts = refs[:count]
    noise, packed, out = refs[count:]
    total = parts[0][...]
    for p in parts[1:]:
        total = total + p[...]
    half = total.shape[1] // 2
    tabs = Tables(None, packed, None, 2 * half, 0)
    sh, sl = split(total)
    e = mm3((sh[:, :half], sl[:, :half]), tabs.fwd(0))
    o = mm3((sh[:, half:], sl[:, half:]), tabs.fwd(1))
    out[:, :half] = e + o - noise[:, :half]
    out[:, half:] = e - o - noise[:, half:]


def local(n, groups, noise, stencil, mean_counts, bias_one, bias_two, owner, depth, counts):
    _, rows, side = noise.shape
    own = noise.reshape(rows, side)
    tiles = side // TC
    slots = counts.shape[1]
    capacity = slots // groups
    backs, packed, reals = [jnp.asarray(t) for t in make_tables(side, rows)]
    vmem = pl.BlockSpec(memory_space=VMEM)
    hbm = pl.BlockSpec(memory_space=pltpu.HBM)

    def swap(value, k, axis="gy", size=n):
        return lax.ppermute(value, axis, [(i, i ^ k) for i in range(size)])

    blocks = {}
    for k in range(n - 2, 0, -2):
        blocks[k] = swap(own, k)
    *msgs, blocks[0] = pl.pallas_call(
        functools.partial(message_kernel, groups, capacity, rows),
        out_shape=[VMEM((capacity, rows + 8, TC), jnp.int32)] * groups
        + [VMEM((rows, side), F32)],
        in_specs=[hbm] * 3,
        out_specs=[vmem] * (groups + 1),
        scratch_shapes=[pltpu.SMEM((slots,), jnp.int32), pltpu.SemaphoreType.DMA((groups + 2,))],
        compiler_params=pltpu.CompilerParams(vmem_limit_bytes=4 * MIB),
        name="messages",
    )(in_hbm(counts.reshape(slots, rows, TC)), in_hbm(depth.reshape(slots)), in_hbm(own))
    for k in range(groups - 1, 0, -1):
        msgs[k] = swap(msgs[k], k, "gx", groups)

    noise_held, backs, packed, reals = lax.optimization_barrier((blocks[0], backs, packed, reals))
    blocks[0] = noise_held
    backs, packed, reals = pl.pallas_call(
        table_kernel,
        out_shape=[VMEM(t.shape, t.dtype) for t in (backs, packed, reals)],
        in_specs=[hbm] * 3,
        out_specs=[vmem] * 3,
        scratch_shapes=[pltpu.SemaphoreType.DMA((3,))],
        compiler_params=pltpu.CompilerParams(vmem_limit_bytes=4 * MIB),
        name="tables",
    )(in_hbm(backs), in_hbm(packed), in_hbm(reals))
    half = side // 2
    ring = rows + PAD
    cell = jax.ShapeDtypeStruct((rows, side), F32)
    along_y = pl.pallas_call(
        functools.partial(along_y_kernel, n, rows, side),
        out_shape=jax.ShapeDtypeStruct((2, half // 2, side), F32),
        in_specs=[vmem] * (n // 2 + 1),
        out_specs=vmem,
        scratch_shapes=[VMEM((2, half // 2, side), BF16)] * 2,
        compiler_params=pltpu.CompilerParams(vmem_limit_bytes=8 * MIB),
        cost_estimate=pl.CostEstimate(flops=1, bytes_accessed=1, transcendentals=0),
        name="along_y",
    )(*[blocks[k] for k in range(0, n, 2)], backs)
    held, msgs[2], msgs[1] = lax.optimization_barrier((along_y, msgs[2], msgs[1]))
    other = swap(held, 1)
    density, smooth, fields = pl.pallas_call(
        functools.partial(field_kernel, n, rows, side),
        out_shape=[cell, VMEM((rows, side), F32), VMEM((5 * ring, side), F32)],
        in_specs=[hbm] + [vmem] * 4,
        out_specs=[vmem] * 3,
        scratch_shapes=[
            *[VMEM((2, half, side), BF16)] * 2,
            *[VMEM((side, 2 * side), BF16)] * 2,
            pltpu.SMEM(stencil.shape, F32),
            pltpu.SemaphoreType.DMA,
        ],
        compiler_params=pltpu.CompilerParams(vmem_limit_bytes=16 * MIB),
        cost_estimate=pl.CostEstimate(flops=1, bytes_accessed=1, transcendentals=0),
        name="fields",
    )(in_hbm(stencil), along_y, other, packed, reals)
    small = (owner.reshape(tiles), stencil, mean_counts, bias_one, bias_two)
    parts = pl.pallas_call(
        functools.partial(adjoint_kernel, n, groups, rows, side, tiles),
        out_shape=[cell] * n,
        in_specs=[hbm] * 5 + [vmem] * (groups + 5),
        out_specs=[vmem] * n,
        scratch_shapes=[
            *[VMEM((2, half, side), BF16)] * 2,
            VMEM((rows, side), F32),
            VMEM((8, side), jnp.int32),
            VMEM((2, half, side), F32),
            *[pltpu.SMEM(a.shape, a.dtype) for a in small],
            pltpu.SemaphoreType.DMA((5,)),
        ],
        compiler_params=pltpu.CompilerParams(vmem_limit_bytes=16 * MIB),
        name="adjoint",
    )(*[in_hbm(a) for a in small], *msgs, smooth, fields, backs, packed, reals)
    sums = {}
    for k in range(n - 2, -1, -2):
        sums[k] = parts[k] + swap(parts[k + 1], 1)
    pieces = [sums[0]] + [swap(sums[k], k) for k in range(n - 2, 0, -2)]
    gradient = pl.pallas_call(
        functools.partial(last_kernel, len(pieces)),
        out_shape=cell,
        in_specs=[vmem] * (len(pieces) + 2),
        out_specs=vmem,
        compiler_params=pltpu.CompilerParams(vmem_limit_bytes=8 * MIB),
        name="sum_and_rows",
    )(*pieces, blocks[0], packed)
    return (gradient.reshape(1, rows, side), density.reshape(1, rows, side))


def solution(mesh):
    return jax.shard_map(
        functools.partial(local, mesh.shape["gy"], mesh.shape["gx"]),
        mesh=mesh,
        in_specs=(
            P("gx", "gy", None),
            P(),
            P(),
            P(),
            P(),
            P("gy", "gx", None, None),
            P("gx", None, "gy"),
            P("gx", None, "gy", None, None),
        ),
        out_specs=(P("gx", "gy", None), P("gx", "gy", None)),
        check_vma=False,
    )
```

```python
import functools
import math

import jax
import jax.numpy as jnp
import ml_dtypes
import numpy as np
from jax import lax
from jax.experimental import pallas as pl
from jax.experimental.pallas import tpu as pltpu
from jax.sharding import PartitionSpec as P

TC = 128
AMPLITUDE = 0.75
PIVOT = 1.0
GROWTH = 7.0 / 8.0
PAD = 16
STENCIL_ROWS = 16
MIB = 1024 * 1024
VMEM = pltpu.VMEM
F32 = jnp.float32
BF16 = jnp.bfloat16


def split_np(table):
    high = table.astype(np.float32).astype(ml_dtypes.bfloat16)
    low = (table - high.astype(np.float64)).astype(np.float32).astype(ml_dtypes.bfloat16)
    return high, low


def make_tables(side, rows):
    half = side // 2
    quarter = side // 4
    freqs = np.concatenate([np.arange(0, half, 2), np.arange(1, half, 2)])
    wave = 2.0 * math.pi / side * freqs

    def basis(cells):
        turn = (freqs[:, None] * cells[None, :]) % side
        angle = 2.0 * math.pi / side * turn
        cos, sin = np.cos(angle), np.sin(angle)
        return np.concatenate([cos[:quarter], sin[:quarter], cos[quarter:], sin[quarter:]])

    def slope(cells):
        turn = (freqs[:, None] * cells[None, :]) % side
        angle = 2.0 * math.pi / side * turn
        cos, sin = -wave[:, None] * np.sin(angle), wave[:, None] * np.cos(angle)
        return np.concatenate([cos[:quarter], sin[:quarter], cos[quarter:], sin[quarter:]])

    plain = basis(np.arange(half))
    even, odd = plain[:half], plain[half:]
    ring = np.concatenate([np.arange(rows + 1), np.zeros(PAD - 2, int), [side - 1]])
    used = np.ones(rows + PAD)
    used[rows + 1 : rows + PAD - 1] = 0.0
    views = np.concatenate([(basis(ring) * used).T, (slope(ring) * used).T])
    wave_sq = wave[:, None] ** 2 + wave[None, :] ** 2
    inverse = np.where(wave_sq > 0, 1.0 / np.where(wave_sq > 0, wave_sq, 1.0), 0.0)
    weight = np.where(freqs == 0, 1.0, 2.0)
    gain = AMPLITUDE * (np.sqrt(wave_sq) / PIVOT) / (1.0 + wave_sq / PIVOT**2)
    gain = gain * weight[:, None] * weight[None, :] / (side * side)
    sections = []
    for table in (even, odd, even.T, odd.T):
        sections.append(np.concatenate(split_np(np.ascontiguousarray(table)), axis=1))
    sections.extend(split_np(views))
    up_h, up_l = split_np(np.ascontiguousarray(views.T))
    lift = np.concatenate([up_h, up_h, up_l], axis=1)
    sections.append(np.concatenate([lift, np.zeros((side, side - lift.shape[1]), lift.dtype)], axis=1))
    waves = np.zeros((8, half))
    waves[:] = wave[None, :]
    return (
        np.concatenate(sections[2:4]),
        np.concatenate(sections[:2] + sections[4:]),
        np.concatenate([gain, inverse, waves]).astype(np.float32),
    )


class Tables:
    def __init__(self, backs, packed, reals, side, ring):
        half = side // 2
        self.half = half
        self.ring = ring
        self.backs = backs
        self.packed = packed
        self.reals = reals
        self.lift_at = 2 * half + 4 * ring

    def fwd(self, par):
        half, at = self.half, par * self.half
        return self.packed[at : at + half, :half], self.packed[at : at + half, half:]

    def back(self, par):
        half, at = self.half, par * self.half
        return self.backs[at : at + half, :half], self.backs[at : at + half, half:]

    def views(self):
        at, count = 2 * self.half, 2 * self.ring
        return self.packed[at : at + count, :], self.packed[at + count : at + 2 * count, :]

    def lift(self, start, count):
        return self.packed[self.lift_at + start : self.lift_at + start + count, : 6 * self.ring]

    def gain(self, par, ypar):
        q = self.half // 2
        return self.reals[par * q : (par + 1) * q, ypar * q : (ypar + 1) * q]

    def inverse(self, par, ypar):
        q, half = self.half // 2, self.half
        return self.reals[half + par * q : half + (par + 1) * q, ypar * q : (ypar + 1) * q]

    def waves(self):
        q, half = self.half // 2, self.half
        row = self.reals[2 * half : 2 * half + 1, :]
        return row[:, :q], row[:, q:]


def mm(a, b):
    return jnp.dot(a, b, preferred_element_type=F32)


def split(a):
    high = a.astype(BF16)
    return high, (a - high.astype(F32)).astype(BF16)


def mm3(a, b):
    count = a[0].shape[0]
    both = mm(jnp.concatenate([a[0], a[1]], axis=0), b[0])
    return both[:count] + (both[count:] + mm(a[0], b[1]))


def turn_rows(a, step):
    return pltpu.roll(a, step % a.shape[0], 0)


def turn_lanes(a, step):
    return pltpu.roll(a, step % a.shape[1], 1)


def slope_lanes(a, waves, orient):
    q = a.shape[1] // 4
    parts = []
    for par in range(2):
        w = waves[par] * orient
        cos, sin = a[:, 2 * par * q : (2 * par + 1) * q], a[:, (2 * par + 1) * q : (2 * par + 2) * q]
        parts.extend([w * sin, -w * cos])
    return jnp.concatenate(parts, axis=1)


def place_of(me, k, n):
    return lax.rem(lax.bitwise_xor(me, k) - me + n, n)


def along_y_kernel(n, rows, side, *refs):
    half = side // 2
    blocks = refs[: n // 2]
    backs, out, fh, fl = refs[n // 2 :]
    tabs = Tables(backs, None, None, side, 0)
    me = lax.axis_index("gy")
    for i in range(n // 4):
        a, b = blocks[i][...], blocks[i + n // 4][...]
        place = place_of(me, 2 * i, n)
        sign = jnp.where(place < n // 2, 1.0, -1.0).astype(F32)
        off = pl.multiple_of(lax.rem(place, n // 2) // 2 * rows, rows)
        for par, v in ((0, a + b), (1, (a - b) * sign)):
            lo, hi = v[:, :half], v[:, half:]
            for ypar, w in ((0, lo + hi), (1, lo - hi)):
                h, l = split(w)
                fh[par, pl.ds(off, rows), ypar * half : (ypar + 1) * half] = h
                fl[par, pl.ds(off, rows), ypar * half : (ypar + 1) * half] = l
    for par in range(2):
        for ypar in range(2):
            cols = slice(ypar * half, (ypar + 1) * half)
            out[par, :, cols] = mm3((fh[par, :, cols], fl[par, :, cols]), tabs.back(ypar))


def field_kernel(n, rows, side, *refs):
    half, q = side // 2, side // 4
    ring = rows + PAD
    values, own, other, packed, reals = refs[:5]
    density_out, smooth_out, fields_out = refs[5:8]
    yh, yl, zh, zl = refs[8:]
    tabs = Tables(None, packed, reals, side, ring)

    odd = lax.rem(lax.axis_index("gy"), 2)
    for i in range(n // 4):
        place = jnp.where(odd == 1, (2 * i - 1) % (n // 2), 2 * i + 1)
        off = pl.multiple_of(place * rows, rows)
        sign = jnp.where(odd == 1, -1.0, 1.0).astype(F32) if i == 0 else 1.0
        rs = slice(i * rows, (i + 1) * rows)
        for par in range(2):
            yh[par, 2 * i * rows : (2 * i + 1) * rows, :], yl[par, 2 * i * rows : (2 * i + 1) * rows, :] = split(
                own[par, rs, :]
            )
            v = other[par, rs, :]
            h, l = split(v * sign if par else v)
            yh[par, pl.ds(off, rows), :] = h
            yl[par, pl.ds(off, rows), :] = l

    for par in range(2):
        for ypar in range(2):
            cols = slice(ypar * half, (ypar + 1) * half)
            x = mm3(tabs.fwd(par), (yh[par, :, cols], yl[par, :, cols]))
            g = tabs.gain(par, ypar)
            inv = tabs.inverse(par, ypar)
            for i in range(2):
                for j in range(2):
                    base = x[i * q : (i + 1) * q, j * q : (j + 1) * q] * g
                    phi = base * inv
                    rs = slice(par * half + i * q, par * half + (i + 1) * q)
                    c0 = ypar * half + j * q
                    zh[rs, c0 : c0 + q], zl[rs, c0 : c0 + q] = split(base)
                    zh[rs, side + c0 : side + c0 + q], zl[rs, side + c0 : side + c0 + q] = split(phi)

    w = mm3(tabs.views(), (zh[...], zl[...]))
    ky = tabs.waves()
    base, base_x = w[:ring, :side], w[ring:, :side]
    phi, phi_x = w[:ring, side:], w[ring:, side:]
    stack = jnp.concatenate([base, phi_x, slope_lanes(phi, ky, 1.0), base_x, slope_lanes(base, ky, 1.0)], axis=0)
    sh, sl = split(stack)
    e = mm3((sh[:, :half], sl[:, :half]), tabs.fwd(0))
    o = mm3((sh[:, half:], sl[:, half:]), tabs.fwd(1))
    fields = jnp.concatenate([e + o, e - o], axis=1)
    fields_out[...] = fields
    linear, shift_x, shift_y, slope_x, slope_y = [fields[i * ring : (i + 1) * ring] for i in range(5)]
    density = linear + GROWTH * linear * linear - (shift_x * slope_x + shift_y * slope_y)
    density_out[...] = density[:rows]

    weights = [values[i : i + 1, :] for i in range(9)]
    beside = {0: density, 1: turn_lanes(density, -1), -1: turn_lanes(density, 1)}
    smooth = jnp.zeros_like(density)
    for a in (-1, 0, 1):
        band = sum(weights[(a + 1) * 3 + b + 1] * beside[b] for b in (-1, 0, 1))
        smooth = smooth + (turn_rows(band, -a) if a else band)
    smooth_out[...] = smooth[:rows]


def adjoint_kernel(n, rows, side, *refs):
    half, q = side // 2, side // 4
    ring = rows + PAD
    values, counts, kinds, smooth_in, fields, density, backs, packed, reals = refs[:9]
    density_out = refs[9]
    outs = refs[10 : 10 + n]
    yh, yl, part, sem = refs[10 + n :]
    tabs = Tables(backs, packed, reals, side, ring)
    ky = tabs.waves()
    me = lax.axis_index("gy")
    leave = pltpu.make_async_copy(density, density_out, sem)
    leave.start()

    smooth = smooth_in[...]
    linear, shift_x, shift_y, slope_x, slope_y = [fields[i * ring : (i + 1) * ring, :] for i in range(5)]
    mean_v, one_v, two_v = [kinds[i * 8 : i * 8 + 1, :] for i in range(3)]
    rate = mean_v * jnp.exp(one_v * smooth + two_v * smooth * smooth)
    score = (counts[...] - rate) * (one_v + 2.0 * two_v * smooth)
    score = jnp.concatenate([score, jnp.zeros((PAD, side), F32)], axis=0)
    weights = [values[i : i + 1, :] for i in range(9)]
    beside = {0: score, 1: turn_lanes(score, 1), -1: turn_lanes(score, -1)}
    pulled = jnp.zeros_like(score)
    for a in (-1, 0, 1):
        band = sum(weights[(a + 1) * 3 + b + 1] * beside[b] for b in (-1, 0, 1))
        pulled = pulled + (turn_rows(band, a) if a else band)

    bars = jnp.concatenate(
        [
            pulled * (1.0 + 2.0 * GROWTH * linear),
            -pulled * slope_x,
            -pulled * slope_y,
            -pulled * shift_x,
            -pulled * shift_y,
        ],
        axis=0,
    )
    lo, hi = bars[:, :half], bars[:, half:]
    ye = mm3(split(lo + hi), tabs.back(0))
    yo = mm3(split(lo - hi), tabs.back(1))
    modes = jnp.concatenate([ye, yo], axis=1)
    m_lin, m_sx, m_sy, m_gx, m_gy = [modes[i * ring : (i + 1) * ring] for i in range(5)]
    to_base = m_lin + slope_lanes(m_gy, ky, -1.0)
    to_phi = slope_lanes(m_sy, ky, -1.0)
    pile = jnp.concatenate(
        [jnp.concatenate([to_base, to_phi], axis=1), jnp.concatenate([m_gx, m_sx], axis=1)], axis=0
    )
    ph, plow = split(pile)
    pile3 = jnp.concatenate([ph, plow, ph], axis=0)

    for par in range(2):
        for i in range(2):
            rs = slice(par * half + i * q, par * half + (i + 1) * q)
            x = mm(tabs.lift(rs.start, q), pile3)
            for ypar in range(2):
                g = tabs.gain(par, ypar)
                inv = tabs.inverse(par, ypar)
                for j in range(2):
                    c0 = ypar * half + j * q
                    d = g * (x[:, c0 : c0 + q] + inv * x[:, side + c0 : side + c0 + q])
                    yh[par, i * q : (i + 1) * q, c0 : c0 + q], yl[par, i * q : (i + 1) * q, c0 : c0 + q] = split(d)
    e = mm3(tabs.back(0), (yh[0], yl[0]))
    o = mm3(tabs.back(1), (yh[1], yl[1]))
    part[0] = e + o
    part[1] = e - o
    for k in range(n):
        place = place_of(me, k, n)
        off = pl.multiple_of(lax.rem(place, n // 2) * rows, rows)
        outs[k][...] = part[place // (n // 2), pl.ds(off, rows), :]
    leave.wait()


def message_kernel(groups, capacity, rows, side, *refs):
    counts, depth, noise, *small = refs[:8]
    msgs = refs[8 : 8 + groups]
    noise_out, picks, values = refs[8 + groups : 11 + groups]
    classes, owner, stencil, *kinds, sems = refs[11 + groups :]
    mine = lax.axis_index("gx")
    heads = [
        pltpu.make_async_copy(a, b, sems.at[i]) for i, (a, b) in enumerate(zip((depth, *small), (classes, owner, stencil, *kinds)))
    ]
    for copy in heads:
        copy.start()
    copies = []
    for k in range(groups):
        start = lax.bitwise_xor(mine, k) * capacity
        copies.append(
            pltpu.make_async_copy(
                counts.at[pl.ds(start * rows, capacity * rows)], msgs[k].at[pl.ds(0, capacity * rows), :], sems.at[6 + k]
            )
        )
    copies.append(pltpu.make_async_copy(noise, noise_out, sems.at[6 + groups]))
    for copy in copies:
        copy.start()
    for copy in heads:
        copy.wait()
    for k in range(groups):
        start = lax.bitwise_xor(mine, k) * capacity
        for r in range(capacity):
            at = capacity * rows + r
            msgs[k][at : at + 1, :] = jnp.full((1, TC), classes[start + r], jnp.int32)
    for t in range(owner.shape[0]):
        rank = jnp.int32(0)
        for t2 in range(t):
            rank = rank + (owner[t2] == owner[t]).astype(jnp.int32)
        pick = lax.bitwise_xor(owner[t], mine) * capacity + rank
        picks[:, t * TC : (t + 1) * TC] = jnp.full((8, TC), pick, jnp.int32)
    for i in range(stencil.shape[0]):
        values[i : i + 1, :] = jnp.full((1, side), stencil[i], F32)
    at = STENCIL_ROWS
    for kind in kinds:
        for d in range(kind.shape[0]):
            values[at : at + 1, :] = jnp.full((1, side), kind[d], F32)
            at += 1
    for copy in copies:
        copy.wait()


def select_kernel(groups, capacity, rows, depths, *refs):
    msgs = refs[:groups][::-1]
    picks, values, counts_out, kinds_out = refs[groups:]
    side = counts_out.shape[1]

    def piece(k, r):
        at = capacity * rows + r
        return msgs[k][r * rows : (r + 1) * rows, :], msgs[k][at : at + 1, :]

    for t in range(side // TC):
        cols = slice(t * TC, (t + 1) * TC)
        pick = picks[:1, cols]
        cells, classes = piece(0, 0)
        for k in range(groups):
            for r in range(capacity):
                if k + r:
                    hit = pick == k * capacity + r
                    more, kind = piece(k, r)
                    cells = jnp.where(hit, more, cells)
                    classes = jnp.where(hit, kind, classes)
        counts_out[:, cols] = cells.astype(F32)
        for i in range(3):
            at = STENCIL_ROWS + i * depths
            value = values[at : at + 1, cols]
            for d in range(1, depths):
                value = jnp.where(classes == d, values[at + d : at + d + 1, cols], value)
            kinds_out[i * 8 : (i + 1) * 8, cols] = jnp.broadcast_to(value, (8, TC))


def table_kernel(*refs):
    sems = refs[-1]
    count = len(refs) // 2
    copies = [pltpu.make_async_copy(refs[i], refs[count + i], sems.at[i]) for i in range(count)]
    for copy in copies:
        copy.start()
    for copy in copies:
        copy.wait()


def in_hbm(value):
    return pltpu.with_memory_space_constraint(value, pltpu.HBM)


def last_kernel(count, *refs):
    parts = refs[:count]
    noise, packed, out = refs[count:]
    total = parts[0][...]
    for p in parts[1:]:
        total = total + p[...]
    half = total.shape[1] // 2
    tabs = Tables(None, packed, None, 2 * half, 0)
    sh, sl = split(total)
    e = mm3((sh[:, :half], sl[:, :half]), tabs.fwd(0))
    o = mm3((sh[:, half:], sl[:, half:]), tabs.fwd(1))
    out[:, :half] = e + o - noise[:, :half]
    out[:, half:] = e - o - noise[:, half:]


def local(n, groups, noise, stencil, mean_counts, bias_one, bias_two, owner, depth, counts):
    _, rows, side = noise.shape
    own = noise.reshape(rows, side)
    tiles = side // TC
    slots = counts.shape[1]
    capacity = slots // groups
    backs, packed, reals = [jnp.asarray(t) for t in make_tables(side, rows)]
    vmem = pl.BlockSpec(memory_space=VMEM)
    hbm = pl.BlockSpec(memory_space=pltpu.HBM)

    def swap(value, k, axis="gy", size=n):
        return lax.ppermute(value, axis, [(i, i ^ k) for i in range(size)])

    blocks = {}
    for k in range(n - 2, 0, -2):
        blocks[k] = swap(own, k)
    small = (owner.reshape(tiles), stencil, mean_counts, bias_one, bias_two)
    depths = mean_counts.shape[0]
    *msgs, blocks[0], picks, values = pl.pallas_call(
        functools.partial(message_kernel, groups, capacity, rows, side),
        out_shape=[VMEM((capacity * rows + 8, TC), jnp.int32)] * groups
        + [
            VMEM((rows, side), F32),
            VMEM((8, side), jnp.int32),
            VMEM((STENCIL_ROWS + -(-3 * depths // 8) * 8, side), F32),
        ],
        in_specs=[hbm] * 8,
        out_specs=[vmem] * (groups + 3),
        scratch_shapes=[
            pltpu.SMEM((slots,), jnp.int32),
            *[pltpu.SMEM(a.shape, a.dtype) for a in small],
            pltpu.SemaphoreType.DMA((groups + 7,)),
        ],
        compiler_params=pltpu.CompilerParams(vmem_limit_bytes=4 * MIB),
        name="messages",
    )(*[in_hbm(a) for a in (counts.reshape(slots * rows, TC), depth.reshape(slots), own, *small)])
    for k in range(groups - 1, 0, -1):
        msgs[k] = swap(msgs[k], k, "gx", groups)

    noise_held, backs, packed, reals = lax.optimization_barrier((blocks[0], backs, packed, reals))
    blocks[0] = noise_held
    backs, packed, reals = pl.pallas_call(
        table_kernel,
        out_shape=[VMEM(t.shape, t.dtype) for t in (backs, packed, reals)],
        in_specs=[hbm] * 3,
        out_specs=[vmem] * 3,
        scratch_shapes=[pltpu.SemaphoreType.DMA((3,))],
        compiler_params=pltpu.CompilerParams(vmem_limit_bytes=4 * MIB),
        name="tables",
    )(in_hbm(backs), in_hbm(packed), in_hbm(reals))
    half = side // 2
    ring = rows + PAD
    cell = jax.ShapeDtypeStruct((rows, side), F32)
    along_y = pl.pallas_call(
        functools.partial(along_y_kernel, n, rows, side),
        out_shape=jax.ShapeDtypeStruct((2, half // 2, side), F32),
        in_specs=[vmem] * (n // 2 + 1),
        out_specs=vmem,
        scratch_shapes=[VMEM((2, half // 2, side), BF16)] * 2,
        compiler_params=pltpu.CompilerParams(vmem_limit_bytes=8 * MIB),
        name="along_y",
    )(*[blocks[k] for k in range(0, n, 2)], backs)
    other = swap(along_y, 1)
    picked, kinds = pl.pallas_call(
        functools.partial(select_kernel, groups, capacity, rows, depths),
        out_shape=[VMEM((rows, side), F32), VMEM((24, side), F32)],
        in_specs=[vmem] * (groups + 2),
        out_specs=[vmem] * 2,
        compiler_params=pltpu.CompilerParams(vmem_limit_bytes=4 * MIB),
        cost_estimate=pl.CostEstimate(flops=20_000_000_000, bytes_accessed=1, transcendentals=0),
        name="select",
    )(*msgs[::-1], picks, values)
    other, picked, kinds = lax.optimization_barrier((other, picked, kinds))
    density, smooth, fields = pl.pallas_call(
        functools.partial(field_kernel, n, rows, side),
        out_shape=[VMEM((rows, side), F32), VMEM((rows, side), F32), VMEM((5 * ring, side), F32)],
        in_specs=[vmem] * 5,
        out_specs=[vmem] * 3,
        scratch_shapes=[
            *[VMEM((2, half, side), BF16)] * 2,
            *[VMEM((side, 2 * side), BF16)] * 2,
        ],
        compiler_params=pltpu.CompilerParams(vmem_limit_bytes=16 * MIB),
        name="fields",
    )(values, along_y, other, packed, reals)
    density, *parts = pl.pallas_call(
        functools.partial(adjoint_kernel, n, rows, side),
        out_shape=[cell] * (1 + n),
        in_specs=[vmem] * 9,
        out_specs=[hbm] + [vmem] * n,
        scratch_shapes=[
            *[VMEM((2, half, side), BF16)] * 2,
            VMEM((2, half, side), F32),
            pltpu.SemaphoreType.DMA,
        ],
        compiler_params=pltpu.CompilerParams(vmem_limit_bytes=16 * MIB),
        name="adjoint",
    )(values, picked, kinds, smooth, fields, density, backs, packed, reals)
    sums = {}
    for k in range(n - 2, -1, -2):
        sums[k] = parts[k] + swap(parts[k + 1], 1)
    pieces = [sums[0]] + [swap(sums[k], k) for k in range(n - 2, 0, -2)]
    gradient = pl.pallas_call(
        functools.partial(last_kernel, len(pieces)),
        out_shape=cell,
        in_specs=[vmem] * (len(pieces) + 2),
        out_specs=vmem,
        compiler_params=pltpu.CompilerParams(vmem_limit_bytes=8 * MIB),
        name="sum_and_rows",
    )(*pieces, blocks[0], packed)
    return (gradient.reshape(1, rows, side), density.reshape(1, rows, side))


def solution(mesh):
    return jax.shard_map(
        functools.partial(local, mesh.shape["gy"], mesh.shape["gx"]),
        mesh=mesh,
        in_specs=(
            P("gx", "gy", None),
            P(),
            P(),
            P(),
            P(),
            P("gy", "gx", None, None),
            P("gx", None, "gy"),
            P("gx", None, "gy", None, None),
        ),
        out_specs=(P("gx", "gy", None), P("gx", "gy", None)),
        check_vma=False,
    )
```

```python
import functools
import math

import jax
import jax.numpy as jnp
import ml_dtypes
import numpy as np
from jax import lax
from jax.experimental import pallas as pl
from jax.experimental.pallas import tpu as pltpu
from jax.sharding import PartitionSpec as P

TC = 128
AMPLITUDE = 0.75
PIVOT = 1.0
GROWTH = 7.0 / 8.0
PAD = 16
STENCIL_ROWS = 16
MIB = 1024 * 1024
VMEM = pltpu.VMEM
F32 = jnp.float32
BF16 = jnp.bfloat16


def split_np(table):
    high = table.astype(np.float32).astype(ml_dtypes.bfloat16)
    low = (table - high.astype(np.float64)).astype(np.float32).astype(ml_dtypes.bfloat16)
    return high, low


def make_tables(side, rows):
    half = side // 2
    quarter = side // 4
    freqs = np.concatenate([np.arange(0, half, 2), np.arange(1, half, 2)])
    wave = 2.0 * math.pi / side * freqs

    def basis(cells):
        turn = (freqs[:, None] * cells[None, :]) % side
        angle = 2.0 * math.pi / side * turn
        cos, sin = np.cos(angle), np.sin(angle)
        return np.concatenate([cos[:quarter], sin[:quarter], cos[quarter:], sin[quarter:]])

    def slope(cells):
        turn = (freqs[:, None] * cells[None, :]) % side
        angle = 2.0 * math.pi / side * turn
        cos, sin = -wave[:, None] * np.sin(angle), wave[:, None] * np.cos(angle)
        return np.concatenate([cos[:quarter], sin[:quarter], cos[quarter:], sin[quarter:]])

    plain = basis(np.arange(half))
    even, odd = plain[:half], plain[half:]
    ring = np.concatenate([np.arange(rows + 1), np.zeros(PAD - 2, int), [side - 1]])
    used = np.ones(rows + PAD)
    used[rows + 1 : rows + PAD - 1] = 0.0
    views = np.concatenate([(basis(ring) * used).T, (slope(ring) * used).T])
    wave_sq = wave[:, None] ** 2 + wave[None, :] ** 2
    inverse = np.where(wave_sq > 0, 1.0 / np.where(wave_sq > 0, wave_sq, 1.0), 0.0)
    weight = np.where(freqs == 0, 1.0, 2.0)
    gain = AMPLITUDE * (np.sqrt(wave_sq) / PIVOT) / (1.0 + wave_sq / PIVOT**2)
    gain = gain * weight[:, None] * weight[None, :] / (side * side)
    sections = []
    for table in (even, odd, even.T, odd.T):
        sections.append(np.concatenate(split_np(np.ascontiguousarray(table)), axis=1))
    sections.extend(split_np(views))
    up_h, up_l = split_np(np.ascontiguousarray(views.T))
    lift = np.concatenate([up_h, up_h, up_l], axis=1)
    sections.append(np.concatenate([lift, np.zeros((side, side - lift.shape[1]), lift.dtype)], axis=1))
    waves = np.zeros((8, half))
    waves[:] = wave[None, :]
    return (
        np.concatenate(sections[2:4]),
        np.concatenate(sections[:2] + sections[4:]),
        np.concatenate([gain, inverse, waves]).astype(np.float32),
    )


class Tables:
    def __init__(self, backs, packed, reals, side, ring):
        half = side // 2
        self.half = half
        self.ring = ring
        self.backs = backs
        self.packed = packed
        self.reals = reals
        self.lift_at = 2 * half + 4 * ring

    def fwd(self, par):
        half, at = self.half, par * self.half
        return self.packed[at : at + half, :half], self.packed[at : at + half, half:]

    def back(self, par):
        half, at = self.half, par * self.half
        return self.backs[at : at + half, :half], self.backs[at : at + half, half:]

    def views(self):
        at, count = 2 * self.half, 2 * self.ring
        return self.packed[at : at + count, :], self.packed[at + count : at + 2 * count, :]

    def lift(self, start, count):
        return self.packed[self.lift_at + start : self.lift_at + start + count, : 6 * self.ring]

    def gain(self, par, ypar):
        q = self.half // 2
        return self.reals[par * q : (par + 1) * q, ypar * q : (ypar + 1) * q]

    def inverse(self, par, ypar):
        q, half = self.half // 2, self.half
        return self.reals[half + par * q : half + (par + 1) * q, ypar * q : (ypar + 1) * q]

    def waves(self):
        q, half = self.half // 2, self.half
        row = self.reals[2 * half : 2 * half + 1, :]
        return row[:, :q], row[:, q:]


def mm(a, b):
    return jnp.dot(a, b, preferred_element_type=F32)


def split(a):
    high = a.astype(BF16)
    return high, (a - high.astype(F32)).astype(BF16)


def mm3(a, b):
    count = a[0].shape[0]
    both = mm(jnp.concatenate([a[0], a[1]], axis=0), b[0])
    return both[:count] + (both[count:] + mm(a[0], b[1]))


def turn_rows(a, step):
    return pltpu.roll(a, step % a.shape[0], 0)


def turn_lanes(a, step):
    return pltpu.roll(a, step % a.shape[1], 1)


def slope_lanes(a, waves, orient):
    q = a.shape[1] // 4
    parts = []
    for par in range(2):
        w = waves[par] * orient
        cos, sin = a[:, 2 * par * q : (2 * par + 1) * q], a[:, (2 * par + 1) * q : (2 * par + 2) * q]
        parts.extend([w * sin, -w * cos])
    return jnp.concatenate(parts, axis=1)


def place_of(me, k, n):
    return lax.rem(lax.bitwise_xor(me, k) - me + n, n)


def along_y_kernel(n, rows, side, *refs):
    half = side // 2
    blocks = refs[: n // 2]
    backs, out, fh, fl = refs[n // 2 :]
    tabs = Tables(backs, None, None, side, 0)
    me = lax.axis_index("gy")
    for i in range(n // 4):
        a, b = blocks[i][...], blocks[i + n // 4][...]
        place = place_of(me, 2 * i, n)
        sign = jnp.where(place < n // 2, 1.0, -1.0).astype(F32)
        off = pl.multiple_of(lax.rem(place, n // 2) // 2 * rows, rows)
        for par, v in ((0, a + b), (1, (a - b) * sign)):
            lo, hi = v[:, :half], v[:, half:]
            for ypar, w in ((0, lo + hi), (1, lo - hi)):
                h, l = split(w)
                fh[par, pl.ds(off, rows), ypar * half : (ypar + 1) * half] = h
                fl[par, pl.ds(off, rows), ypar * half : (ypar + 1) * half] = l
    for par in range(2):
        for ypar in range(2):
            cols = slice(ypar * half, (ypar + 1) * half)
            out[par, :, cols] = mm3((fh[par, :, cols], fl[par, :, cols]), tabs.back(ypar))


def field_kernel(n, rows, side, *refs):
    half, q = side // 2, side // 4
    ring = rows + PAD
    values, own, other, packed, reals = refs[:5]
    density_out, smooth_out, fields_out = refs[5:8]
    yh, yl, zh, zl = refs[8:]
    tabs = Tables(None, packed, reals, side, ring)

    odd = lax.rem(lax.axis_index("gy"), 2)
    for i in range(n // 4):
        place = jnp.where(odd == 1, (2 * i - 1) % (n // 2), 2 * i + 1)
        off = pl.multiple_of(place * rows, rows)
        sign = jnp.where(odd == 1, -1.0, 1.0).astype(F32) if i == 0 else 1.0
        rs = slice(i * rows, (i + 1) * rows)
        for par in range(2):
            yh[par, 2 * i * rows : (2 * i + 1) * rows, :], yl[par, 2 * i * rows : (2 * i + 1) * rows, :] = split(
                own[par, rs, :]
            )
            v = other[par, rs, :]
            h, l = split(v * sign if par else v)
            yh[par, pl.ds(off, rows), :] = h
            yl[par, pl.ds(off, rows), :] = l

    for par in range(2):
        for ypar in range(2):
            cols = slice(ypar * half, (ypar + 1) * half)
            x = mm3(tabs.fwd(par), (yh[par, :, cols], yl[par, :, cols]))
            g = tabs.gain(par, ypar)
            inv = tabs.inverse(par, ypar)
            for i in range(2):
                for j in range(2):
                    base = x[i * q : (i + 1) * q, j * q : (j + 1) * q] * g
                    phi = base * inv
                    rs = slice(par * half + i * q, par * half + (i + 1) * q)
                    c0 = ypar * half + j * q
                    zh[rs, c0 : c0 + q], zl[rs, c0 : c0 + q] = split(base)
                    zh[rs, side + c0 : side + c0 + q], zl[rs, side + c0 : side + c0 + q] = split(phi)

    w = mm3(tabs.views(), (zh[...], zl[...]))
    ky = tabs.waves()
    base, base_x = w[:ring, :side], w[ring:, :side]
    phi, phi_x = w[:ring, side:], w[ring:, side:]
    stack = jnp.concatenate([base, phi_x, slope_lanes(phi, ky, 1.0), base_x, slope_lanes(base, ky, 1.0)], axis=0)
    sh, sl = split(stack)
    e = mm3((sh[:, :half], sl[:, :half]), tabs.fwd(0))
    o = mm3((sh[:, half:], sl[:, half:]), tabs.fwd(1))
    fields = jnp.concatenate([e + o, e - o], axis=1)
    fields_out[...] = fields
    linear, shift_x, shift_y, slope_x, slope_y = [fields[i * ring : (i + 1) * ring] for i in range(5)]
    density = linear + GROWTH * linear * linear - (shift_x * slope_x + shift_y * slope_y)
    density_out[...] = density[:rows]

    weights = [values[i : i + 1, :] for i in range(9)]
    beside = {0: density, 1: turn_lanes(density, -1), -1: turn_lanes(density, 1)}
    smooth = jnp.zeros_like(density)
    for a in (-1, 0, 1):
        band = sum(weights[(a + 1) * 3 + b + 1] * beside[b] for b in (-1, 0, 1))
        smooth = smooth + (turn_rows(band, -a) if a else band)
    smooth_out[...] = smooth[:rows]


def adjoint_kernel(n, rows, side, *refs):
    half, q = side // 2, side // 4
    ring = rows + PAD
    values, counts, kinds, smooth_in, fields, density, backs, packed, reals = refs[:9]
    density_out = refs[9]
    outs = refs[10 : 10 + n]
    yh, yl, part, sem = refs[10 + n :]
    tabs = Tables(backs, packed, reals, side, ring)
    ky = tabs.waves()
    me = lax.axis_index("gy")
    leave = pltpu.make_async_copy(density, density_out, sem)
    leave.start()

    smooth = smooth_in[...]
    linear, shift_x, shift_y, slope_x, slope_y = [fields[i * ring : (i + 1) * ring, :] for i in range(5)]
    mean_v, one_v, two_v = [kinds[i * 8 : i * 8 + 1, :] for i in range(3)]
    rate = mean_v * jnp.exp(one_v * smooth + two_v * smooth * smooth)
    score = (counts[...] - rate) * (one_v + 2.0 * two_v * smooth)
    score = jnp.concatenate([score, jnp.zeros((PAD, side), F32)], axis=0)
    weights = [values[i : i + 1, :] for i in range(9)]
    beside = {0: score, 1: turn_lanes(score, 1), -1: turn_lanes(score, -1)}
    pulled = jnp.zeros_like(score)
    for a in (-1, 0, 1):
        band = sum(weights[(a + 1) * 3 + b + 1] * beside[b] for b in (-1, 0, 1))
        pulled = pulled + (turn_rows(band, a) if a else band)

    bars = jnp.concatenate(
        [
            pulled * (1.0 + 2.0 * GROWTH * linear),
            -pulled * slope_x,
            -pulled * slope_y,
            -pulled * shift_x,
            -pulled * shift_y,
        ],
        axis=0,
    )
    lo, hi = bars[:, :half], bars[:, half:]
    ye = mm3(split(lo + hi), tabs.back(0))
    yo = mm3(split(lo - hi), tabs.back(1))
    modes = jnp.concatenate([ye, yo], axis=1)
    m_lin, m_sx, m_sy, m_gx, m_gy = [modes[i * ring : (i + 1) * ring] for i in range(5)]
    to_base = m_lin + slope_lanes(m_gy, ky, -1.0)
    to_phi = slope_lanes(m_sy, ky, -1.0)
    pile = jnp.concatenate(
        [jnp.concatenate([to_base, to_phi], axis=1), jnp.concatenate([m_gx, m_sx], axis=1)], axis=0
    )
    ph, plow = split(pile)
    pile3 = jnp.concatenate([ph, plow, ph], axis=0)

    for par in range(2):
        for i in range(2):
            rs = slice(par * half + i * q, par * half + (i + 1) * q)
            x = mm(tabs.lift(rs.start, q), pile3)
            for ypar in range(2):
                g = tabs.gain(par, ypar)
                inv = tabs.inverse(par, ypar)
                for j in range(2):
                    c0 = ypar * half + j * q
                    d = g * (x[:, c0 : c0 + q] + inv * x[:, side + c0 : side + c0 + q])
                    yh[par, i * q : (i + 1) * q, c0 : c0 + q], yl[par, i * q : (i + 1) * q, c0 : c0 + q] = split(d)
    e = mm3(tabs.back(0), (yh[0], yl[0]))
    o = mm3(tabs.back(1), (yh[1], yl[1]))
    part[0] = e + o
    part[1] = e - o
    for k in range(n):
        place = place_of(me, k, n)
        off = pl.multiple_of(lax.rem(place, n // 2) * rows, rows)
        outs[k][...] = part[place // (n // 2), pl.ds(off, rows), :]
    leave.wait()


def message_kernel(groups, capacity, rows, side, *refs):
    counts, noise, backs, depth, *small = refs[:9]
    msgs = refs[9 : 9 + groups]
    noise_out, backs_out, picks, values = refs[9 + groups : 13 + groups]
    classes, owner, stencil, *kinds, sems = refs[13 + groups :]
    mine = lax.axis_index("gx")
    heads = [
        pltpu.make_async_copy(a, b, sems.at[i]) for i, (a, b) in enumerate(zip((depth, *small), (classes, owner, stencil, *kinds)))
    ]
    for copy in heads:
        copy.start()
    copies = []
    for k in range(groups):
        start = lax.bitwise_xor(mine, k) * capacity
        copies.append(
            pltpu.make_async_copy(
                counts.at[pl.ds(start * rows, capacity * rows)], msgs[k].at[pl.ds(0, capacity * rows), :], sems.at[6 + k]
            )
        )
    copies.append(pltpu.make_async_copy(noise, noise_out, sems.at[6 + groups]))
    copies.append(pltpu.make_async_copy(backs, backs_out, sems.at[7 + groups]))
    for copy in copies:
        copy.start()
    for copy in heads:
        copy.wait()
    for k in range(groups):
        start = lax.bitwise_xor(mine, k) * capacity
        for r in range(capacity):
            at = capacity * rows + r
            msgs[k][at : at + 1, :] = jnp.full((1, TC), classes[start + r], jnp.int32)
    for t in range(owner.shape[0]):
        rank = jnp.int32(0)
        for t2 in range(t):
            rank = rank + (owner[t2] == owner[t]).astype(jnp.int32)
        pick = lax.bitwise_xor(owner[t], mine) * capacity + rank
        picks[:, t * TC : (t + 1) * TC] = jnp.full((8, TC), pick, jnp.int32)
    for i in range(stencil.shape[0]):
        values[i : i + 1, :] = jnp.full((1, side), stencil[i], F32)
    at = STENCIL_ROWS
    for kind in kinds:
        for d in range(kind.shape[0]):
            values[at : at + 1, :] = jnp.full((1, side), kind[d], F32)
            at += 1
    for copy in copies:
        copy.wait()


def select_kernel(groups, capacity, rows, depths, *refs):
    msgs = refs[:groups][::-1]
    picks, values, counts_out, kinds_out = refs[groups:]
    side = counts_out.shape[1]

    def piece(k, r):
        at = capacity * rows + r
        return msgs[k][r * rows : (r + 1) * rows, :], msgs[k][at : at + 1, :]

    for t in range(side // TC):
        cols = slice(t * TC, (t + 1) * TC)
        pick = picks[:1, cols]
        cells, classes = piece(0, 0)
        for k in range(groups):
            for r in range(capacity):
                if k + r:
                    hit = pick == k * capacity + r
                    more, kind = piece(k, r)
                    cells = jnp.where(hit, more, cells)
                    classes = jnp.where(hit, kind, classes)
        counts_out[:, cols] = cells.astype(F32)
        for i in range(3):
            at = STENCIL_ROWS + i * depths
            value = values[at : at + 1, cols]
            for d in range(1, depths):
                value = jnp.where(classes == d, values[at + d : at + d + 1, cols], value)
            kinds_out[i * 8 : (i + 1) * 8, cols] = jnp.broadcast_to(value, (8, TC))


def table_kernel(*refs):
    sems = refs[-1]
    count = len(refs) // 2
    copies = [pltpu.make_async_copy(refs[i], refs[count + i], sems.at[i]) for i in range(count)]
    for copy in copies:
        copy.start()
    for copy in copies:
        copy.wait()


def in_hbm(value):
    return pltpu.with_memory_space_constraint(value, pltpu.HBM)


def last_kernel(count, *refs):
    parts = refs[:count]
    noise, packed, out = refs[count:]
    total = parts[0][...]
    for p in parts[1:]:
        total = total + p[...]
    half = total.shape[1] // 2
    tabs = Tables(None, packed, None, 2 * half, 0)
    sh, sl = split(total)
    e = mm3((sh[:, :half], sl[:, :half]), tabs.fwd(0))
    o = mm3((sh[:, half:], sl[:, half:]), tabs.fwd(1))
    out[:, :half] = e + o - noise[:, :half]
    out[:, half:] = e - o - noise[:, half:]


def local(n, groups, noise, stencil, mean_counts, bias_one, bias_two, owner, depth, counts):
    _, rows, side = noise.shape
    own = noise.reshape(rows, side)
    tiles = side // TC
    slots = counts.shape[1]
    capacity = slots // groups
    backs, packed, reals = [jnp.asarray(t) for t in make_tables(side, rows)]
    vmem = pl.BlockSpec(memory_space=VMEM)
    hbm = pl.BlockSpec(memory_space=pltpu.HBM)

    def swap(value, k, axis="gy", size=n):
        return lax.ppermute(value, axis, [(i, i ^ k) for i in range(size)])

    blocks = {}
    for k in range(n - 2, 0, -2):
        blocks[k] = swap(own, k)
    small = (owner.reshape(tiles), stencil, mean_counts, bias_one, bias_two)
    depths = mean_counts.shape[0]
    *msgs, blocks[0], backs, picks, values = pl.pallas_call(
        functools.partial(message_kernel, groups, capacity, rows, side),
        out_shape=[VMEM((capacity * rows + 8, TC), jnp.int32)] * groups
        + [
            VMEM((rows, side), F32),
            VMEM(backs.shape, backs.dtype),
            VMEM((8, side), jnp.int32),
            VMEM((STENCIL_ROWS + -(-3 * depths // 8) * 8, side), F32),
        ],
        in_specs=[hbm] * 9,
        out_specs=[vmem] * (groups + 4),
        scratch_shapes=[
            pltpu.SMEM((slots,), jnp.int32),
            *[pltpu.SMEM(a.shape, a.dtype) for a in small],
            pltpu.SemaphoreType.DMA((groups + 8,)),
        ],
        compiler_params=pltpu.CompilerParams(vmem_limit_bytes=4 * MIB),
        name="messages",
    )(*[in_hbm(a) for a in (counts.reshape(slots * rows, TC), own, backs, depth.reshape(slots), *small)])
    for k in range(groups - 1, 0, -1):
        msgs[k] = swap(msgs[k], k, "gx", groups)

    half = side // 2
    ring = rows + PAD
    cell = jax.ShapeDtypeStruct((rows, side), F32)
    along_y = pl.pallas_call(
        functools.partial(along_y_kernel, n, rows, side),
        out_shape=jax.ShapeDtypeStruct((2, half // 2, side), F32),
        in_specs=[vmem] * (n // 2 + 1),
        out_specs=vmem,
        scratch_shapes=[VMEM((2, half // 2, side), BF16)] * 2,
        compiler_params=pltpu.CompilerParams(vmem_limit_bytes=8 * MIB),
        name="along_y",
    )(*[blocks[k] for k in range(0, n, 2)], backs)
    other = swap(along_y, 1)
    packed, reals, _ = lax.optimization_barrier((packed, reals, along_y))
    packed, reals = pl.pallas_call(
        table_kernel,
        out_shape=[VMEM(t.shape, t.dtype) for t in (packed, reals)],
        in_specs=[hbm] * 2,
        out_specs=[vmem] * 2,
        scratch_shapes=[pltpu.SemaphoreType.DMA((2,))],
        compiler_params=pltpu.CompilerParams(vmem_limit_bytes=4 * MIB),
        cost_estimate=pl.CostEstimate(flops=20_000_000_000, bytes_accessed=1, transcendentals=0),
        name="tables",
    )(in_hbm(packed), in_hbm(reals))
    density, smooth, fields = pl.pallas_call(
        functools.partial(field_kernel, n, rows, side),
        out_shape=[VMEM((rows, side), F32), VMEM((rows, side), F32), VMEM((5 * ring, side), F32)],
        in_specs=[vmem] * 5,
        out_specs=[vmem] * 3,
        scratch_shapes=[
            *[VMEM((2, half, side), BF16)] * 2,
            *[VMEM((side, 2 * side), BF16)] * 2,
        ],
        compiler_params=pltpu.CompilerParams(vmem_limit_bytes=16 * MIB),
        name="fields",
    )(values, along_y, other, packed, reals)
    picks, smooth = lax.optimization_barrier((picks, smooth))
    picked, kinds = pl.pallas_call(
        functools.partial(select_kernel, groups, capacity, rows, depths),
        out_shape=[VMEM((rows, side), F32), VMEM((24, side), F32)],
        in_specs=[vmem] * (groups + 2),
        out_specs=[vmem] * 2,
        compiler_params=pltpu.CompilerParams(vmem_limit_bytes=4 * MIB),
        name="select",
    )(*msgs[::-1], picks, values)
    density, *parts = pl.pallas_call(
        functools.partial(adjoint_kernel, n, rows, side),
        out_shape=[cell] * (1 + n),
        in_specs=[vmem] * 9,
        out_specs=[hbm] + [vmem] * n,
        scratch_shapes=[
            *[VMEM((2, half, side), BF16)] * 2,
            VMEM((2, half, side), F32),
            pltpu.SemaphoreType.DMA,
        ],
        compiler_params=pltpu.CompilerParams(vmem_limit_bytes=16 * MIB),
        name="adjoint",
    )(values, picked, kinds, smooth, fields, density, backs, packed, reals)
    sums = {}
    for k in range(n - 2, -1, -2):
        sums[k] = parts[k] + swap(parts[k + 1], 1)
    pieces = [sums[0]] + [swap(sums[k], k) for k in range(n - 2, 0, -2)]
    gradient = pl.pallas_call(
        functools.partial(last_kernel, len(pieces)),
        out_shape=cell,
        in_specs=[vmem] * (len(pieces) + 2),
        out_specs=vmem,
        compiler_params=pltpu.CompilerParams(vmem_limit_bytes=8 * MIB),
        name="sum_and_rows",
    )(*pieces, blocks[0], packed)
    return (gradient.reshape(1, rows, side), density.reshape(1, rows, side))


def solution(mesh):
    return jax.shard_map(
        functools.partial(local, mesh.shape["gy"], mesh.shape["gx"]),
        mesh=mesh,
        in_specs=(
            P("gx", "gy", None),
            P(),
            P(),
            P(),
            P(),
            P("gy", "gx", None, None),
            P("gx", None, "gy"),
            P("gx", None, "gy", None, None),
        ),
        out_specs=(P("gx", "gy", None), P("gx", "gy", None)),
        check_vma=False,
    )
```

```python
import functools
import math

import jax
import jax.numpy as jnp
import ml_dtypes
import numpy as np
from jax import lax
from jax.experimental import pallas as pl
from jax.experimental.pallas import tpu as pltpu
from jax.sharding import PartitionSpec as P

TC = 128
AMPLITUDE = 0.75
PIVOT = 1.0
GROWTH = 7.0 / 8.0
PAD = 16
STENCIL_ROWS = 16
MIB = 1024 * 1024
VMEM = pltpu.VMEM
F32 = jnp.float32
BF16 = jnp.bfloat16


def split_np(table):
    high = table.astype(np.float32).astype(ml_dtypes.bfloat16)
    low = (table - high.astype(np.float64)).astype(np.float32).astype(ml_dtypes.bfloat16)
    return high, low


def make_tables(side, rows):
    half = side // 2
    quarter = side // 4
    freqs = np.concatenate([np.arange(0, half, 2), np.arange(1, half, 2)])
    wave = 2.0 * math.pi / side * freqs

    def basis(cells):
        turn = (freqs[:, None] * cells[None, :]) % side
        angle = 2.0 * math.pi / side * turn
        cos, sin = np.cos(angle), np.sin(angle)
        return np.concatenate([cos[:quarter], sin[:quarter], cos[quarter:], sin[quarter:]])

    def slope(cells):
        turn = (freqs[:, None] * cells[None, :]) % side
        angle = 2.0 * math.pi / side * turn
        cos, sin = -wave[:, None] * np.sin(angle), wave[:, None] * np.cos(angle)
        return np.concatenate([cos[:quarter], sin[:quarter], cos[quarter:], sin[quarter:]])

    plain = basis(np.arange(half))
    even, odd = plain[:half], plain[half:]
    ring = np.concatenate([np.arange(rows + 1), np.zeros(PAD - 2, int), [side - 1]])
    used = np.ones(rows + PAD)
    used[rows + 1 : rows + PAD - 1] = 0.0
    plain_rows, slope_rows = (basis(ring) * used).T, (slope(ring) * used).T
    twice = np.repeat(wave.reshape(2, 1, quarter), 2, axis=1).reshape(-1) ** 2
    views = np.concatenate([plain_rows, slope_rows, plain_rows * twice, slope_rows * twice])
    up = np.concatenate([plain_rows, slope_rows]).T
    wave_sq = wave[:, None] ** 2 + wave[None, :] ** 2
    inverse = np.where(wave_sq > 0, 1.0 / np.where(wave_sq > 0, wave_sq, 1.0), 0.0)
    weight = np.where(freqs == 0, 1.0, 2.0)
    gain = AMPLITUDE * (np.sqrt(wave_sq) / PIVOT) / (1.0 + wave_sq / PIVOT**2)
    gain = gain * weight[:, None] * weight[None, :] / (side * side)
    sections = []
    for table in (even, odd, even.T, odd.T):
        sections.append(np.concatenate(split_np(np.ascontiguousarray(table)), axis=1))
    sections.extend(split_np(views))
    up_h, up_l = split_np(np.ascontiguousarray(up))
    lift = np.concatenate([up_h, up_h, up_l], axis=1)
    sections.append(np.concatenate([lift, np.zeros((side, side - lift.shape[1]), lift.dtype)], axis=1))
    waves = np.zeros((8, half))
    waves[:] = wave[None, :]
    return (
        np.concatenate(sections[2:4]),
        np.concatenate(sections[:2] + sections[4:]),
        np.concatenate([gain, gain * inverse, waves]).astype(np.float32),
    )


class Tables:
    def __init__(self, backs, packed, reals, side, ring):
        half = side // 2
        self.half = half
        self.ring = ring
        self.backs = backs
        self.packed = packed
        self.reals = reals
        self.lift_at = 2 * half + 8 * ring

    def fwd(self, par):
        half, at = self.half, par * self.half
        return self.packed[at : at + half, :half], self.packed[at : at + half, half:]

    def back(self, par):
        half, at = self.half, par * self.half
        return self.backs[at : at + half, :half], self.backs[at : at + half, half:]

    def views(self):
        at, count = 2 * self.half, 4 * self.ring
        return self.packed[at : at + count, :], self.packed[at + count : at + 2 * count, :]

    def lift(self, start, count):
        return self.packed[self.lift_at + start : self.lift_at + start + count, : 6 * self.ring]

    def gain(self, par, ypar):
        q = self.half // 2
        return self.reals[par * q : (par + 1) * q, ypar * q : (ypar + 1) * q]

    def gain_phi(self, par, ypar):
        q, half = self.half // 2, self.half
        return self.reals[half + par * q : half + (par + 1) * q, ypar * q : (ypar + 1) * q]

    def waves(self):
        q, half = self.half // 2, self.half
        row = self.reals[2 * half : 2 * half + 1, :]
        return row[:, :q], row[:, q:]


def mm(a, b):
    return jnp.dot(a, b, preferred_element_type=F32)


def split(a):
    high = a.astype(BF16)
    return high, (a - high.astype(F32)).astype(BF16)


def mm3(a, b):
    count = a[0].shape[0]
    both = mm(jnp.concatenate([a[0], a[1]], axis=0), b[0])
    return both[:count] + (both[count:] + mm(a[0], b[1]))


def turn_rows(a, step):
    return pltpu.roll(a, step % a.shape[0], 0)


def turn_lanes(a, step):
    return pltpu.roll(a, step % a.shape[1], 1)


def slope_lanes(a, waves, orient):
    q = a.shape[1] // 4
    parts = []
    for par in range(2):
        w = waves[par] * orient
        cos, sin = a[:, 2 * par * q : (2 * par + 1) * q], a[:, (2 * par + 1) * q : (2 * par + 2) * q]
        parts.extend([w * sin, -w * cos])
    return jnp.concatenate(parts, axis=1)


def place_of(me, k, n):
    return lax.rem(lax.bitwise_xor(me, k) - me + n, n)


def along_y_kernel(n, rows, side, *refs):
    half = side // 2
    blocks = refs[: n // 2]
    backs, out, fh, fl = refs[n // 2 :]
    tabs = Tables(backs, None, None, side, 0)
    me = lax.axis_index("gy")
    for i in range(n // 4):
        a, b = blocks[i][...], blocks[i + n // 4][...]
        place = place_of(me, 2 * i, n)
        sign = jnp.where(place < n // 2, 1.0, -1.0).astype(F32)
        off = pl.multiple_of(lax.rem(place, n // 2) // 2 * rows, rows)
        for par, v in ((0, a + b), (1, (a - b) * sign)):
            lo, hi = v[:, :half], v[:, half:]
            for ypar, w in ((0, lo + hi), (1, lo - hi)):
                h, l = split(w)
                fh[par, pl.ds(off, rows), ypar * half : (ypar + 1) * half] = h
                fl[par, pl.ds(off, rows), ypar * half : (ypar + 1) * half] = l
    for par in range(2):
        for ypar in range(2):
            cols = slice(ypar * half, (ypar + 1) * half)
            out[par, :, cols] = mm3((fh[par, :, cols], fl[par, :, cols]), tabs.back(ypar))


def field_kernel(n, rows, side, *refs):
    half, q = side // 2, side // 4
    ring = rows + PAD
    values, own, other, packed, reals = refs[:5]
    density_out, smooth_out, fields_out = refs[5:8]
    yh, yl, zh, zl = refs[8:]
    tabs = Tables(None, packed, reals, side, ring)

    odd = lax.rem(lax.axis_index("gy"), 2)
    for i in range(n // 4):
        place = jnp.where(odd == 1, (2 * i - 1) % (n // 2), 2 * i + 1)
        off = pl.multiple_of(place * rows, rows)
        sign = jnp.where(odd == 1, -1.0, 1.0).astype(F32) if i == 0 else 1.0
        rs = slice(i * rows, (i + 1) * rows)
        for par in range(2):
            yh[par, 2 * i * rows : (2 * i + 1) * rows, :], yl[par, 2 * i * rows : (2 * i + 1) * rows, :] = split(
                own[par, rs, :]
            )
            v = other[par, rs, :]
            h, l = split(v * sign if par else v)
            yh[par, pl.ds(off, rows), :] = h
            yl[par, pl.ds(off, rows), :] = l

    for par in range(2):
        for ypar in range(2):
            cols = slice(ypar * half, (ypar + 1) * half)
            x = mm3(tabs.fwd(par), (yh[par, :, cols], yl[par, :, cols]))
            g = tabs.gain_phi(par, ypar)
            for i in range(2):
                for j in range(2):
                    phi = x[i * q : (i + 1) * q, j * q : (j + 1) * q] * g
                    rs = slice(par * half + i * q, par * half + (i + 1) * q)
                    c0 = ypar * half + j * q
                    zh[rs, c0 : c0 + q], zl[rs, c0 : c0 + q] = split(phi)

    w = mm3(tabs.views(), (zh[...], zl[...]))
    ky = tabs.waves()
    ky_sq = jnp.concatenate([ky[0] * ky[0]] * 2 + [ky[1] * ky[1]] * 2, axis=1)
    phi, phi_x, base, base_x = [w[i * ring : (i + 1) * ring] for i in range(4)]
    base, base_x = base + ky_sq * phi, base_x + ky_sq * phi_x
    stack = jnp.concatenate([base, phi_x, slope_lanes(phi, ky, 1.0), base_x, slope_lanes(base, ky, 1.0)], axis=0)
    sh, sl = split(stack)
    e = mm3((sh[:, :half], sl[:, :half]), tabs.fwd(0))
    o = mm3((sh[:, half:], sl[:, half:]), tabs.fwd(1))
    fields = jnp.concatenate([e + o, e - o], axis=1)
    fields_out[...] = fields
    linear, shift_x, shift_y, slope_x, slope_y = [fields[i * ring : (i + 1) * ring] for i in range(5)]
    density = linear + GROWTH * linear * linear - (shift_x * slope_x + shift_y * slope_y)
    density_out[...] = density[:rows]

    weights = [values[i : i + 1, :] for i in range(9)]
    beside = {0: density, 1: turn_lanes(density, -1), -1: turn_lanes(density, 1)}
    smooth = jnp.zeros_like(density)
    for a in (-1, 0, 1):
        band = sum(weights[(a + 1) * 3 + b + 1] * beside[b] for b in (-1, 0, 1))
        smooth = smooth + (turn_rows(band, -a) if a else band)
    smooth_out[...] = smooth[:rows]


def adjoint_kernel(n, rows, side, *refs):
    half, q = side // 2, side // 4
    ring = rows + PAD
    values, counts, kinds, smooth_in, fields, density, backs, packed, reals = refs[:9]
    density_out = refs[9]
    outs = refs[10 : 10 + n]
    yh, yl, part, sem = refs[10 + n :]
    tabs = Tables(backs, packed, reals, side, ring)
    ky = tabs.waves()
    me = lax.axis_index("gy")
    leave = pltpu.make_async_copy(density, density_out, sem)
    leave.start()

    smooth = smooth_in[...]
    linear, shift_x, shift_y, slope_x, slope_y = [fields[i * ring : (i + 1) * ring, :] for i in range(5)]
    mean_v, one_v, two_v = [kinds[i * 8 : i * 8 + 1, :] for i in range(3)]
    rate = mean_v * jnp.exp(one_v * smooth + two_v * smooth * smooth)
    score = (counts[...] - rate) * (one_v + 2.0 * two_v * smooth)
    score = jnp.concatenate([score, jnp.zeros((PAD, side), F32)], axis=0)
    weights = [values[i : i + 1, :] for i in range(9)]
    beside = {0: score, 1: turn_lanes(score, 1), -1: turn_lanes(score, -1)}
    pulled = jnp.zeros_like(score)
    for a in (-1, 0, 1):
        band = sum(weights[(a + 1) * 3 + b + 1] * beside[b] for b in (-1, 0, 1))
        pulled = pulled + (turn_rows(band, a) if a else band)

    bars = jnp.concatenate(
        [
            pulled * (1.0 + 2.0 * GROWTH * linear),
            -pulled * slope_x,
            -pulled * slope_y,
            -pulled * shift_x,
            -pulled * shift_y,
        ],
        axis=0,
    )
    lo, hi = bars[:, :half], bars[:, half:]
    ye = mm3(split(lo + hi), tabs.back(0))
    yo = mm3(split(lo - hi), tabs.back(1))
    modes = jnp.concatenate([ye, yo], axis=1)
    m_lin, m_sx, m_sy, m_gx, m_gy = [modes[i * ring : (i + 1) * ring] for i in range(5)]
    to_base = m_lin + slope_lanes(m_gy, ky, -1.0)
    to_phi = slope_lanes(m_sy, ky, -1.0)
    pile = jnp.concatenate(
        [jnp.concatenate([to_base, to_phi], axis=1), jnp.concatenate([m_gx, m_sx], axis=1)], axis=0
    )
    ph, plow = split(pile)
    pile3 = jnp.concatenate([ph, plow, ph], axis=0)

    for par in range(2):
        for i in range(2):
            rs = slice(par * half + i * q, par * half + (i + 1) * q)
            x = mm(tabs.lift(rs.start, q), pile3)
            for ypar in range(2):
                g = tabs.gain(par, ypar)
                g_phi = tabs.gain_phi(par, ypar)
                for j in range(2):
                    c0 = ypar * half + j * q
                    d = g * x[:, c0 : c0 + q] + g_phi * x[:, side + c0 : side + c0 + q]
                    yh[par, i * q : (i + 1) * q, c0 : c0 + q], yl[par, i * q : (i + 1) * q, c0 : c0 + q] = split(d)
    e = mm3(tabs.back(0), (yh[0], yl[0]))
    o = mm3(tabs.back(1), (yh[1], yl[1]))
    part[0] = e + o
    part[1] = e - o
    for k in range(n):
        place = place_of(me, k, n)
        off = pl.multiple_of(lax.rem(place, n // 2) * rows, rows)
        outs[k][...] = part[place // (n // 2), pl.ds(off, rows), :]
    leave.wait()


def message_kernel(groups, capacity, rows, side, *refs):
    counts, noise, backs, depth, *small = refs[:9]
    msgs = refs[9 : 9 + groups]
    noise_out, backs_out, picks, values = refs[9 + groups : 13 + groups]
    classes, owner, stencil, *kinds, sems = refs[13 + groups :]
    mine = lax.axis_index("gx")
    heads = [
        pltpu.make_async_copy(a, b, sems.at[i]) for i, (a, b) in enumerate(zip((depth, *small), (classes, owner, stencil, *kinds)))
    ]
    for copy in heads:
        copy.start()
    copies = []
    for k in range(groups):
        start = lax.bitwise_xor(mine, k) * capacity
        copies.append(
            pltpu.make_async_copy(
                counts.at[pl.ds(start * rows, capacity * rows)], msgs[k].at[pl.ds(0, capacity * rows), :], sems.at[6 + k]
            )
        )
    copies.append(pltpu.make_async_copy(noise, noise_out, sems.at[6 + groups]))
    copies.append(pltpu.make_async_copy(backs, backs_out, sems.at[7 + groups]))
    for copy in copies:
        copy.start()
    for copy in heads:
        copy.wait()
    for k in range(groups):
        start = lax.bitwise_xor(mine, k) * capacity
        for r in range(capacity):
            at = capacity * rows + r
            msgs[k][at : at + 1, :] = jnp.full((1, TC), classes[start + r], jnp.int32)
    for t in range(owner.shape[0]):
        rank = jnp.int32(0)
        for t2 in range(t):
            rank = rank + (owner[t2] == owner[t]).astype(jnp.int32)
        pick = lax.bitwise_xor(owner[t], mine) * capacity + rank
        picks[:, t * TC : (t + 1) * TC] = jnp.full((8, TC), pick, jnp.int32)
    for i in range(stencil.shape[0]):
        values[i : i + 1, :] = jnp.full((1, side), stencil[i], F32)
    at = STENCIL_ROWS
    for kind in kinds:
        for d in range(kind.shape[0]):
            values[at : at + 1, :] = jnp.full((1, side), kind[d], F32)
            at += 1
    for copy in copies:
        copy.wait()


def arrival_order(groups):
    first = (2, 3, 1)
    return list(first) + [k for k in range(groups) if k not in first]


def select_kernel(groups, capacity, rows, depths, *refs):
    msgs = dict(zip(arrival_order(groups), refs[:groups]))
    picks, values, counts_out, kinds_out = refs[groups:]
    side = counts_out.shape[1]

    def piece(k, r):
        at = capacity * rows + r
        return msgs[k][r * rows : (r + 1) * rows, :], msgs[k][at : at + 1, :]

    for t in range(side // TC):
        cols = slice(t * TC, (t + 1) * TC)
        pick = picks[:1, cols]
        cells, classes = piece(0, 0)
        for k in range(groups):
            for r in range(capacity):
                if k + r:
                    hit = pick == k * capacity + r
                    more, kind = piece(k, r)
                    cells = jnp.where(hit, more, cells)
                    classes = jnp.where(hit, kind, classes)
        counts_out[:, cols] = cells.astype(F32)
        for i in range(3):
            at = STENCIL_ROWS + i * depths
            value = values[at : at + 1, cols]
            for d in range(1, depths):
                value = jnp.where(classes == d, values[at + d : at + d + 1, cols], value)
            kinds_out[i * 8 : (i + 1) * 8, cols] = jnp.broadcast_to(value, (8, TC))


def table_kernel(*refs):
    sems = refs[-1]
    count = len(refs) // 2
    copies = [pltpu.make_async_copy(refs[i], refs[count + i], sems.at[i]) for i in range(count)]
    for copy in copies:
        copy.start()
    for copy in copies:
        copy.wait()


def in_hbm(value):
    return pltpu.with_memory_space_constraint(value, pltpu.HBM)


def last_kernel(count, *refs):
    parts = refs[:count]
    noise, packed, out = refs[count:]
    total = parts[0][...]
    for p in parts[1:]:
        total = total + p[...]
    half = total.shape[1] // 2
    tabs = Tables(None, packed, None, 2 * half, 0)
    sh, sl = split(total)
    e = mm3((sh[:, :half], sl[:, :half]), tabs.fwd(0))
    o = mm3((sh[:, half:], sl[:, half:]), tabs.fwd(1))
    out[:, :half] = e + o - noise[:, :half]
    out[:, half:] = e - o - noise[:, half:]


def local(n, groups, noise, stencil, mean_counts, bias_one, bias_two, owner, depth, counts):
    _, rows, side = noise.shape
    own = noise.reshape(rows, side)
    tiles = side // TC
    slots = counts.shape[1]
    capacity = slots // groups
    backs, packed, reals = [jnp.asarray(t) for t in make_tables(side, rows)]
    vmem = pl.BlockSpec(memory_space=VMEM)
    hbm = pl.BlockSpec(memory_space=pltpu.HBM)

    def swap(value, k, axis="gy", size=n):
        return lax.ppermute(value, axis, [(i, i ^ k) for i in range(size)])

    blocks = {}
    for k in range(n - 2, 0, -2):
        blocks[k] = swap(own, k)
    small = (owner.reshape(tiles), stencil, mean_counts, bias_one, bias_two)
    depths = mean_counts.shape[0]
    *msgs, blocks[0], backs, picks, values = pl.pallas_call(
        functools.partial(message_kernel, groups, capacity, rows, side),
        out_shape=[VMEM((capacity * rows + 8, TC), jnp.int32)] * groups
        + [
            VMEM((rows, side), F32),
            VMEM(backs.shape, backs.dtype),
            VMEM((8, side), jnp.int32),
            VMEM((STENCIL_ROWS + -(-3 * depths // 8) * 8, side), F32),
        ],
        in_specs=[hbm] * 9,
        out_specs=[vmem] * (groups + 4),
        scratch_shapes=[
            pltpu.SMEM((slots,), jnp.int32),
            *[pltpu.SMEM(a.shape, a.dtype) for a in small],
            pltpu.SemaphoreType.DMA((groups + 8,)),
        ],
        compiler_params=pltpu.CompilerParams(vmem_limit_bytes=4 * MIB),
        name="messages",
    )(*[in_hbm(a) for a in (counts.reshape(slots * rows, TC), own, backs, depth.reshape(slots), *small)])
    for k in range(groups - 1, 0, -1):
        msgs[k] = swap(msgs[k], k, "gx", groups)

    half = side // 2
    ring = rows + PAD
    cell = jax.ShapeDtypeStruct((rows, side), F32)
    along_y = pl.pallas_call(
        functools.partial(along_y_kernel, n, rows, side),
        out_shape=jax.ShapeDtypeStruct((2, half // 2, side), F32),
        in_specs=[vmem] * (n // 2 + 1),
        out_specs=vmem,
        scratch_shapes=[VMEM((2, half // 2, side), BF16)] * 2,
        compiler_params=pltpu.CompilerParams(vmem_limit_bytes=8 * MIB),
        name="along_y",
    )(*[blocks[k] for k in range(0, n, 2)], backs)
    other = swap(along_y, 1)
    packed, reals, _ = lax.optimization_barrier((packed, reals, along_y))
    packed, reals = pl.pallas_call(
        table_kernel,
        out_shape=[VMEM(t.shape, t.dtype) for t in (packed, reals)],
        in_specs=[hbm] * 2,
        out_specs=[vmem] * 2,
        scratch_shapes=[pltpu.SemaphoreType.DMA((2,))],
        compiler_params=pltpu.CompilerParams(vmem_limit_bytes=4 * MIB),
        cost_estimate=pl.CostEstimate(flops=20_000_000_000, bytes_accessed=1, transcendentals=0),
        name="tables",
    )(in_hbm(packed), in_hbm(reals))
    density, smooth, fields = pl.pallas_call(
        functools.partial(field_kernel, n, rows, side),
        out_shape=[VMEM((rows, side), F32), VMEM((rows, side), F32), VMEM((5 * ring, side), F32)],
        in_specs=[vmem] * 5,
        out_specs=[vmem] * 3,
        scratch_shapes=[
            *[VMEM((2, half, side), BF16)] * 2,
            *[VMEM((side, side), BF16)] * 2,
        ],
        compiler_params=pltpu.CompilerParams(vmem_limit_bytes=16 * MIB),
        name="fields",
    )(values, along_y, other, packed, reals)
    picks, smooth = lax.optimization_barrier((picks, smooth))
    picked, kinds = pl.pallas_call(
        functools.partial(select_kernel, groups, capacity, rows, depths),
        out_shape=[VMEM((rows, side), F32), VMEM((24, side), F32)],
        in_specs=[vmem] * (groups + 2),
        out_specs=[vmem] * 2,
        compiler_params=pltpu.CompilerParams(vmem_limit_bytes=4 * MIB),
        name="select",
    )(*[msgs[k] for k in arrival_order(groups)], picks, values)
    density, *parts = pl.pallas_call(
        functools.partial(adjoint_kernel, n, rows, side),
        out_shape=[cell] * (1 + n),
        in_specs=[vmem] * 9,
        out_specs=[hbm] + [vmem] * n,
        scratch_shapes=[
            *[VMEM((2, half, side), BF16)] * 2,
            VMEM((2, half, side), F32),
            pltpu.SemaphoreType.DMA,
        ],
        compiler_params=pltpu.CompilerParams(vmem_limit_bytes=16 * MIB),
        name="adjoint",
    )(values, picked, kinds, smooth, fields, density, backs, packed, reals)
    sums = {}
    for k in range(n - 2, -1, -2):
        sums[k] = parts[k] + swap(parts[k + 1], 1)
    pieces = [sums[0]] + [swap(sums[k], k) for k in range(n - 2, 0, -2)]
    gradient = pl.pallas_call(
        functools.partial(last_kernel, len(pieces)),
        out_shape=cell,
        in_specs=[vmem] * (len(pieces) + 2),
        out_specs=vmem,
        compiler_params=pltpu.CompilerParams(vmem_limit_bytes=8 * MIB),
        name="sum_and_rows",
    )(*pieces, blocks[0], packed)
    return (gradient.reshape(1, rows, side), density.reshape(1, rows, side))


def solution(mesh):
    return jax.shard_map(
        functools.partial(local, mesh.shape["gy"], mesh.shape["gx"]),
        mesh=mesh,
        in_specs=(
            P("gx", "gy", None),
            P(),
            P(),
            P(),
            P(),
            P("gy", "gx", None, None),
            P("gx", None, "gy"),
            P("gx", None, "gy", None, None),
        ),
        out_specs=(P("gx", "gy", None), P("gx", "gy", None)),
        check_vma=False,
    )
```

```python
import functools
import math

import jax
import jax.numpy as jnp
import ml_dtypes
import numpy as np
from jax import lax
from jax.experimental import pallas as pl
from jax.experimental.pallas import tpu as pltpu
from jax.sharding import PartitionSpec as P

TC = 128
AMPLITUDE = 0.75
PIVOT = 1.0
GROWTH = 7.0 / 8.0
PAD = 16
STENCIL_ROWS = 16
MIB = 1024 * 1024
VMEM = pltpu.VMEM
F32 = jnp.float32
BF16 = jnp.bfloat16


def split_np(table):
    high = table.astype(np.float32).astype(ml_dtypes.bfloat16)
    low = (table - high.astype(np.float64)).astype(np.float32).astype(ml_dtypes.bfloat16)
    return high, low


def make_tables(side, rows):
    half = side // 2
    quarter = side // 4
    freqs = np.concatenate([np.arange(0, half, 2), np.arange(1, half, 2)])
    wave = 2.0 * math.pi / side * freqs

    def basis(cells):
        turn = (freqs[:, None] * cells[None, :]) % side
        angle = 2.0 * math.pi / side * turn
        cos, sin = np.cos(angle), np.sin(angle)
        return np.concatenate([cos[:quarter], sin[:quarter], cos[quarter:], sin[quarter:]])

    def slope(cells):
        turn = (freqs[:, None] * cells[None, :]) % side
        angle = 2.0 * math.pi / side * turn
        cos, sin = -wave[:, None] * np.sin(angle), wave[:, None] * np.cos(angle)
        return np.concatenate([cos[:quarter], sin[:quarter], cos[quarter:], sin[quarter:]])

    plain = basis(np.arange(half))
    even, odd = plain[:half], plain[half:]
    ring = np.concatenate([np.arange(rows + 1), np.zeros(PAD - 2, int), [side - 1]])
    used = np.ones(rows + PAD)
    used[rows + 1 : rows + PAD - 1] = 0.0
    plain_rows, slope_rows = (basis(ring) * used).T, (slope(ring) * used).T
    twice = np.repeat(wave.reshape(2, 1, quarter), 2, axis=1).reshape(-1) ** 2
    views = np.concatenate([plain_rows, slope_rows, plain_rows * twice, slope_rows * twice])
    up = np.concatenate([plain_rows, slope_rows]).T
    wave_sq = wave[:, None] ** 2 + wave[None, :] ** 2
    inverse = np.where(wave_sq > 0, 1.0 / np.where(wave_sq > 0, wave_sq, 1.0), 0.0)
    weight = np.where(freqs == 0, 1.0, 2.0)
    gain = AMPLITUDE * (np.sqrt(wave_sq) / PIVOT) / (1.0 + wave_sq / PIVOT**2)
    gain = gain * weight[:, None] * weight[None, :] / (side * side)
    sections = []
    for table in (even, odd, even.T, odd.T):
        sections.append(np.concatenate(split_np(np.ascontiguousarray(table)), axis=1))
    sections.extend(split_np(views))
    up_h, up_l = split_np(np.ascontiguousarray(up))
    lift = np.concatenate([up_h, up_h, up_l], axis=1)
    sections.append(np.concatenate([lift, np.zeros((side, side - lift.shape[1]), lift.dtype)], axis=1))
    waves = np.zeros((8, half))
    waves[:] = wave[None, :]
    return (
        np.concatenate(sections[2:4]),
        np.concatenate(sections[:2] + sections[4:]),
        np.concatenate([gain, gain * inverse, waves]).astype(np.float32),
    )


class Tables:
    def __init__(self, backs, packed, reals, side, ring):
        half = side // 2
        self.half = half
        self.ring = ring
        self.backs = backs
        self.packed = packed
        self.reals = reals
        self.lift_at = 2 * half + 8 * ring

    def fwd(self, par):
        half, at = self.half, par * self.half
        return self.packed[at : at + half, :half], self.packed[at : at + half, half:]

    def back(self, par):
        half, at = self.half, par * self.half
        return self.backs[at : at + half, :half], self.backs[at : at + half, half:]

    def views(self):
        at, count = 2 * self.half, 4 * self.ring
        return self.packed[at : at + count, :], self.packed[at + count : at + 2 * count, :]

    def lift(self, start, count):
        return self.packed[self.lift_at + start : self.lift_at + start + count, : 6 * self.ring]

    def gain(self, par, ypar):
        q = self.half // 2
        return self.reals[par * q : (par + 1) * q, ypar * q : (ypar + 1) * q]

    def gain_phi(self, par, ypar):
        q, half = self.half // 2, self.half
        return self.reals[half + par * q : half + (par + 1) * q, ypar * q : (ypar + 1) * q]

    def waves(self):
        q, half = self.half // 2, self.half
        row = self.reals[2 * half : 2 * half + 1, :]
        return row[:, :q], row[:, q:]


def mm(a, b):
    return jnp.dot(a, b, preferred_element_type=F32)


def split(a):
    high = a.astype(BF16)
    return high, (a - high.astype(F32)).astype(BF16)


def mm3(a, b):
    count = a[0].shape[0]
    both = mm(jnp.concatenate([a[0], a[1]], axis=0), b[0])
    return both[:count] + (both[count:] + mm(a[0], b[1]))


def turn_rows(a, step):
    return pltpu.roll(a, step % a.shape[0], 0)


def turn_lanes(a, step):
    return pltpu.roll(a, step % a.shape[1], 1)


def slope_lanes(a, waves, orient):
    q = a.shape[1] // 4
    parts = []
    for par in range(2):
        w = waves[par] * orient
        cos, sin = a[:, 2 * par * q : (2 * par + 1) * q], a[:, (2 * par + 1) * q : (2 * par + 2) * q]
        parts.extend([w * sin, -w * cos])
    return jnp.concatenate(parts, axis=1)


def place_of(me, k, n):
    return lax.rem(lax.bitwise_xor(me, k) - me + n, n)


def along_y_kernel(n, rows, side, *refs):
    half = side // 2
    blocks = refs[: n // 2]
    backs, out, fh, fl = refs[n // 2 :]
    tabs = Tables(backs, None, None, side, 0)
    me = lax.axis_index("gy")
    for i in range(n // 4):
        a, b = blocks[i][...], blocks[i + n // 4][...]
        place = place_of(me, 2 * i, n)
        sign = jnp.where(place < n // 2, 1.0, -1.0).astype(F32)
        off = pl.multiple_of(lax.rem(place, n // 2) // 2 * rows, rows)
        for par, v in ((0, a + b), (1, (a - b) * sign)):
            lo, hi = v[:, :half], v[:, half:]
            for ypar, w in ((0, lo + hi), (1, lo - hi)):
                h, l = split(w)
                fh[par, pl.ds(off, rows), ypar * half : (ypar + 1) * half] = h
                fl[par, pl.ds(off, rows), ypar * half : (ypar + 1) * half] = l
    for par in range(2):
        for ypar in range(2):
            cols = slice(ypar * half, (ypar + 1) * half)
            out[par, :, cols] = mm3((fh[par, :, cols], fl[par, :, cols]), tabs.back(ypar))


def field_kernel(n, rows, side, *refs):
    half, q = side // 2, side // 4
    ring = rows + PAD
    values, own, other, packed, reals = refs[:5]
    density_out, smooth_out, fields_out = refs[5:8]
    yh, yl, zh, zl = refs[8:]
    tabs = Tables(None, packed, reals, side, ring)

    odd = lax.rem(lax.axis_index("gy"), 2)
    for i in range(n // 4):
        place = jnp.where(odd == 1, (2 * i - 1) % (n // 2), 2 * i + 1)
        off = pl.multiple_of(place * rows, rows)
        sign = jnp.where(odd == 1, -1.0, 1.0).astype(F32) if i == 0 else 1.0
        rs = slice(i * rows, (i + 1) * rows)
        for par in range(2):
            yh[par, 2 * i * rows : (2 * i + 1) * rows, :], yl[par, 2 * i * rows : (2 * i + 1) * rows, :] = split(
                own[par, rs, :]
            )
            v = other[par, rs, :]
            h, l = split(v * sign if par else v)
            yh[par, pl.ds(off, rows), :] = h
            yl[par, pl.ds(off, rows), :] = l

    for par in range(2):
        for ypar in range(2):
            cols = slice(ypar * half, (ypar + 1) * half)
            x = mm3(tabs.fwd(par), (yh[par, :, cols], yl[par, :, cols]))
            g = tabs.gain_phi(par, ypar)
            for i in range(2):
                for j in range(2):
                    phi = x[i * q : (i + 1) * q, j * q : (j + 1) * q] * g
                    rs = slice(par * half + i * q, par * half + (i + 1) * q)
                    c0 = ypar * half + j * q
                    zh[rs, c0 : c0 + q], zl[rs, c0 : c0 + q] = split(phi)

    w = mm3(tabs.views(), (zh[...], zl[...]))
    ky = tabs.waves()
    ky_sq = jnp.concatenate([ky[0] * ky[0]] * 2 + [ky[1] * ky[1]] * 2, axis=1)
    phi, phi_x, base, base_x = [w[i * ring : (i + 1) * ring] for i in range(4)]
    base, base_x = base + ky_sq * phi, base_x + ky_sq * phi_x
    stack = jnp.concatenate([base, phi_x, slope_lanes(phi, ky, 1.0), base_x, slope_lanes(base, ky, 1.0)], axis=0)
    sh, sl = split(stack)
    e = mm3((sh[:, :half], sl[:, :half]), tabs.fwd(0))
    o = mm3((sh[:, half:], sl[:, half:]), tabs.fwd(1))
    fields = jnp.concatenate([e + o, e - o], axis=1)
    fields_out[...] = fields
    linear, shift_x, shift_y, slope_x, slope_y = [fields[i * ring : (i + 1) * ring] for i in range(5)]
    density = linear + GROWTH * linear * linear - (shift_x * slope_x + shift_y * slope_y)
    density_out[...] = density[:rows]

    weights = [values[i : i + 1, :] for i in range(9)]
    beside = {0: density, 1: turn_lanes(density, -1), -1: turn_lanes(density, 1)}
    smooth = jnp.zeros_like(density)
    for a in (-1, 0, 1):
        band = sum(weights[(a + 1) * 3 + b + 1] * beside[b] for b in (-1, 0, 1))
        smooth = smooth + (turn_rows(band, -a) if a else band)
    smooth_out[...] = smooth[:rows]


def adjoint_kernel(n, rows, side, *refs):
    half, q = side // 2, side // 4
    ring = rows + PAD
    values, counts, kinds, smooth_in, fields, density, backs, packed, reals = refs[:9]
    density_out = refs[9]
    outs = refs[10 : 10 + n]
    yh, yl, part, sem = refs[10 + n :]
    tabs = Tables(backs, packed, reals, side, ring)
    ky = tabs.waves()
    me = lax.axis_index("gy")
    leave = pltpu.make_async_copy(density, density_out, sem)
    leave.start()

    smooth = smooth_in[...]
    linear, shift_x, shift_y, slope_x, slope_y = [fields[i * ring : (i + 1) * ring, :] for i in range(5)]
    mean_v, one_v, two_v = [kinds[i * 8 : i * 8 + 1, :] for i in range(3)]
    rate = mean_v * jnp.exp(one_v * smooth + two_v * smooth * smooth)
    score = (counts[...] - rate) * (one_v + 2.0 * two_v * smooth)
    score = jnp.concatenate([score, jnp.zeros((PAD, side), F32)], axis=0)
    weights = [values[i : i + 1, :] for i in range(9)]
    beside = {0: score, 1: turn_lanes(score, 1), -1: turn_lanes(score, -1)}
    pulled = jnp.zeros_like(score)
    for a in (-1, 0, 1):
        band = sum(weights[(a + 1) * 3 + b + 1] * beside[b] for b in (-1, 0, 1))
        pulled = pulled + (turn_rows(band, a) if a else band)

    bars = jnp.concatenate(
        [
            pulled * (1.0 + 2.0 * GROWTH * linear),
            -pulled * slope_x,
            -pulled * slope_y,
            -pulled * shift_x,
            -pulled * shift_y,
        ],
        axis=0,
    )
    lo, hi = bars[:, :half], bars[:, half:]
    ye = mm3(split(lo + hi), tabs.back(0))
    yo = mm3(split(lo - hi), tabs.back(1))
    modes = jnp.concatenate([ye, yo], axis=1)
    m_lin, m_sx, m_sy, m_gx, m_gy = [modes[i * ring : (i + 1) * ring] for i in range(5)]
    to_base = m_lin + slope_lanes(m_gy, ky, -1.0)
    to_phi = slope_lanes(m_sy, ky, -1.0)
    pile = jnp.concatenate(
        [jnp.concatenate([to_base, to_phi], axis=1), jnp.concatenate([m_gx, m_sx], axis=1)], axis=0
    )
    ph, plow = split(pile)
    pile3 = jnp.concatenate([ph, plow, ph], axis=0)

    for par in range(2):
        for i in range(2):
            rs = slice(par * half + i * q, par * half + (i + 1) * q)
            x = mm(tabs.lift(rs.start, q), pile3)
            for ypar in range(2):
                g = tabs.gain(par, ypar)
                g_phi = tabs.gain_phi(par, ypar)
                for j in range(2):
                    c0 = ypar * half + j * q
                    d = g * x[:, c0 : c0 + q] + g_phi * x[:, side + c0 : side + c0 + q]
                    yh[par, i * q : (i + 1) * q, c0 : c0 + q], yl[par, i * q : (i + 1) * q, c0 : c0 + q] = split(d)
    e = mm3(tabs.back(0), (yh[0], yl[0]))
    o = mm3(tabs.back(1), (yh[1], yl[1]))
    part[0] = e + o
    part[1] = e - o
    for k in range(n):
        place = place_of(me, k, n)
        off = pl.multiple_of(lax.rem(place, n // 2) * rows, rows)
        outs[k][...] = part[place // (n // 2), pl.ds(off, rows), :]
    leave.wait()


def message_kernel(groups, capacity, rows, *refs):
    counts, noise, backs, depth = refs[:4]
    msgs = refs[4 : 4 + groups]
    noise_out, backs_out, classes, sems = refs[4 + groups :]
    mine = lax.axis_index("gx")
    head = pltpu.make_async_copy(depth, classes, sems.at[groups])
    head.start()
    copies = []
    for k in range(groups):
        start = lax.bitwise_xor(mine, k) * capacity
        copies.append(
            pltpu.make_async_copy(
                counts.at[pl.ds(start * rows, capacity * rows)], msgs[k].at[pl.ds(0, capacity * rows), :], sems.at[k]
            )
        )
    copies.append(pltpu.make_async_copy(noise, noise_out, sems.at[groups + 1]))
    copies.append(pltpu.make_async_copy(backs, backs_out, sems.at[groups + 2]))
    for copy in copies:
        copy.start()
    head.wait()
    for k in range(groups):
        start = lax.bitwise_xor(mine, k) * capacity
        for r in range(capacity):
            at = capacity * rows + r
            msgs[k][at : at + 1, :] = jnp.full((1, TC), classes[start + r], jnp.int32)
    for copy in copies:
        copy.wait()


def arrival_order(groups):
    first = [k for k in (2, 3, 1) if k < groups]
    return first + [k for k in range(groups) if k not in first]


def select_kernel(groups, capacity, rows, depths, *refs):
    msgs = dict(zip(arrival_order(groups), refs[:groups]))
    picks, values, counts_out, kinds_out = refs[groups:]
    side = counts_out.shape[1]

    def piece(k, r):
        at = capacity * rows + r
        return msgs[k][r * rows : (r + 1) * rows, :], msgs[k][at : at + 1, :]

    for t in range(side // TC):
        cols = slice(t * TC, (t + 1) * TC)
        pick = picks[:1, cols]
        cells, classes = piece(0, 0)
        for k in range(groups):
            for r in range(capacity):
                if k + r:
                    hit = pick == k * capacity + r
                    more, kind = piece(k, r)
                    cells = jnp.where(hit, more, cells)
                    classes = jnp.where(hit, kind, classes)
        counts_out[:, cols] = cells.astype(F32)
        for i in range(3):
            at = STENCIL_ROWS + i * depths
            value = values[at : at + 1, cols]
            for d in range(1, depths):
                value = jnp.where(classes == d, values[at + d : at + d + 1, cols], value)
            kinds_out[i * 8 : (i + 1) * 8, cols] = jnp.broadcast_to(value, (8, TC))


def table_kernel(capacity, count, *refs):
    small, (*tables, picks, values) = refs[: 5 + count], refs[5 + count : 7 + 2 * count]
    owner, stencil, *kinds, sems = refs[7 + 2 * count :]
    side = values.shape[1]
    mine = lax.axis_index("gx")
    copies = [
        pltpu.make_async_copy(a, b, sems.at[i])
        for i, (a, b) in enumerate(zip(small, (owner, stencil, *kinds, *tables)))
    ]
    for copy in copies:
        copy.start()
    for copy in copies[:5]:
        copy.wait()
    for t in range(owner.shape[0]):
        rank = jnp.int32(0)
        for t2 in range(t):
            rank = rank + (owner[t2] == owner[t]).astype(jnp.int32)
        pick = lax.bitwise_xor(owner[t], mine) * capacity + rank
        picks[:, t * TC : (t + 1) * TC] = jnp.full((8, TC), pick, jnp.int32)
    for i in range(stencil.shape[0]):
        values[i : i + 1, :] = jnp.full((1, side), stencil[i], F32)
    at = STENCIL_ROWS
    for kind in kinds:
        for d in range(kind.shape[0]):
            values[at : at + 1, :] = jnp.full((1, side), kind[d], F32)
            at += 1
    for copy in copies[5:]:
        copy.wait()


def in_hbm(value):
    return pltpu.with_memory_space_constraint(value, pltpu.HBM)


def last_kernel(count, *refs):
    parts = refs[:count]
    noise, packed, out = refs[count:]
    total = parts[0][...]
    for p in parts[1:]:
        total = total + p[...]
    half = total.shape[1] // 2
    tabs = Tables(None, packed, None, 2 * half, 0)
    sh, sl = split(total)
    e = mm3((sh[:, :half], sl[:, :half]), tabs.fwd(0))
    o = mm3((sh[:, half:], sl[:, half:]), tabs.fwd(1))
    out[:, :half] = e + o - noise[:, :half]
    out[:, half:] = e - o - noise[:, half:]


def local(n, groups, noise, stencil, mean_counts, bias_one, bias_two, owner, depth, counts):
    _, rows, side = noise.shape
    own = noise.reshape(rows, side)
    tiles = side // TC
    slots = counts.shape[1]
    capacity = slots // groups
    backs, packed, reals = [jnp.asarray(t) for t in make_tables(side, rows)]
    vmem = pl.BlockSpec(memory_space=VMEM)
    hbm = pl.BlockSpec(memory_space=pltpu.HBM)

    def swap(value, k, axis="gy", size=n):
        return lax.ppermute(value, axis, [(i, i ^ k) for i in range(size)])

    blocks = {}
    for k in range(n - 2, 0, -2):
        blocks[k] = swap(own, k)
    small = (owner.reshape(tiles), stencil, mean_counts, bias_one, bias_two)
    depths = mean_counts.shape[0]
    *msgs, blocks[0], backs = pl.pallas_call(
        functools.partial(message_kernel, groups, capacity, rows),
        out_shape=[VMEM((capacity * rows + 8, TC), jnp.int32)] * groups
        + [VMEM((rows, side), F32), VMEM(backs.shape, backs.dtype)],
        in_specs=[hbm] * 4,
        out_specs=[vmem] * (groups + 2),
        scratch_shapes=[pltpu.SMEM((slots,), jnp.int32), pltpu.SemaphoreType.DMA((groups + 3,))],
        compiler_params=pltpu.CompilerParams(vmem_limit_bytes=4 * MIB),
        name="messages",
    )(*[in_hbm(a) for a in (counts.reshape(slots * rows, TC), own, backs, depth.reshape(slots))])
    for k in range(groups - 1, 0, -1):
        msgs[k] = swap(msgs[k], k, "gx", groups)

    half = side // 2
    ring = rows + PAD
    cell = jax.ShapeDtypeStruct((rows, side), F32)
    along_y = pl.pallas_call(
        functools.partial(along_y_kernel, n, rows, side),
        out_shape=jax.ShapeDtypeStruct((2, half // 2, side), F32),
        in_specs=[vmem] * (n // 2 + 1),
        out_specs=vmem,
        scratch_shapes=[VMEM((2, half // 2, side), BF16)] * 2,
        compiler_params=pltpu.CompilerParams(vmem_limit_bytes=8 * MIB),
        name="along_y",
    )(*[blocks[k] for k in range(0, n, 2)], backs)
    other = swap(along_y, 1)
    packed, reals, _ = lax.optimization_barrier((packed, reals, along_y))
    small = (owner.reshape(tiles), stencil, mean_counts, bias_one, bias_two)
    depths = mean_counts.shape[0]
    packed, reals, picks, values = pl.pallas_call(
        functools.partial(table_kernel, capacity, 2),
        out_shape=[
            VMEM(packed.shape, packed.dtype),
            VMEM(reals.shape, reals.dtype),
            VMEM((8, side), jnp.int32),
            VMEM((STENCIL_ROWS + -(-3 * depths // 8) * 8, side), F32),
        ],
        in_specs=[hbm] * 7,
        out_specs=[vmem] * 4,
        scratch_shapes=[*[pltpu.SMEM(a.shape, a.dtype) for a in small], pltpu.SemaphoreType.DMA((7,))],
        compiler_params=pltpu.CompilerParams(vmem_limit_bytes=4 * MIB),
        cost_estimate=pl.CostEstimate(flops=20_000_000_000, bytes_accessed=1, transcendentals=0),
        name="tables",
    )(*[in_hbm(a) for a in (*small, packed, reals)])
    density, smooth, fields = pl.pallas_call(
        functools.partial(field_kernel, n, rows, side),
        out_shape=[VMEM((rows, side), F32), VMEM((rows, side), F32), VMEM((5 * ring, side), F32)],
        in_specs=[vmem] * 5,
        out_specs=[vmem] * 3,
        scratch_shapes=[
            *[VMEM((2, half, side), BF16)] * 2,
            *[VMEM((side, side), BF16)] * 2,
        ],
        compiler_params=pltpu.CompilerParams(vmem_limit_bytes=16 * MIB),
        name="fields",
    )(values, along_y, other, packed, reals)
    picks, smooth = lax.optimization_barrier((picks, smooth))
    picked, kinds = pl.pallas_call(
        functools.partial(select_kernel, groups, capacity, rows, depths),
        out_shape=[VMEM((rows, side), F32), VMEM((24, side), F32)],
        in_specs=[vmem] * (groups + 2),
        out_specs=[vmem] * 2,
        compiler_params=pltpu.CompilerParams(vmem_limit_bytes=4 * MIB),
        name="select",
    )(*[msgs[k] for k in arrival_order(groups)], picks, values)
    density, *parts = pl.pallas_call(
        functools.partial(adjoint_kernel, n, rows, side),
        out_shape=[cell] * (1 + n),
        in_specs=[vmem] * 9,
        out_specs=[hbm] + [vmem] * n,
        scratch_shapes=[
            *[VMEM((2, half, side), BF16)] * 2,
            VMEM((2, half, side), F32),
            pltpu.SemaphoreType.DMA,
        ],
        compiler_params=pltpu.CompilerParams(vmem_limit_bytes=16 * MIB),
        name="adjoint",
    )(values, picked, kinds, smooth, fields, density, backs, packed, reals)
    sums = {}
    for k in range(n - 2, -1, -2):
        sums[k] = parts[k] + swap(parts[k + 1], 1)
    pieces = [sums[0]] + [swap(sums[k], k) for k in range(n - 2, 0, -2)]
    gradient = pl.pallas_call(
        functools.partial(last_kernel, len(pieces)),
        out_shape=cell,
        in_specs=[vmem] * (len(pieces) + 2),
        out_specs=vmem,
        compiler_params=pltpu.CompilerParams(vmem_limit_bytes=8 * MIB),
        name="sum_and_rows",
    )(*pieces, blocks[0], packed)
    return (gradient.reshape(1, rows, side), density.reshape(1, rows, side))


def solution(mesh):
    return jax.shard_map(
        functools.partial(local, mesh.shape["gy"], mesh.shape["gx"]),
        mesh=mesh,
        in_specs=(
            P("gx", "gy", None),
            P(),
            P(),
            P(),
            P(),
            P("gy", "gx", None, None),
            P("gx", None, "gy"),
            P("gx", None, "gy", None, None),
        ),
        out_specs=(P("gx", "gy", None), P("gx", "gy", None)),
        check_vma=False,
    )
```

```python
import functools
import math

import jax
import jax.numpy as jnp
import ml_dtypes
import numpy as np
from jax import lax
from jax.experimental import pallas as pl
from jax.experimental.pallas import tpu as pltpu
from jax.sharding import PartitionSpec as P

TC = 128
AMPLITUDE = 0.75
PIVOT = 1.0
GROWTH = 7.0 / 8.0
PAD = 8
STENCIL_ROWS = 16
MIB = 1024 * 1024
VMEM = pltpu.VMEM
F32 = jnp.float32
BF16 = jnp.bfloat16


def split_np(table):
    high = table.astype(np.float32).astype(ml_dtypes.bfloat16)
    low = (table - high.astype(np.float64)).astype(np.float32).astype(ml_dtypes.bfloat16)
    return high, low


def make_tables(side, rows):
    half = side // 2
    quarter = side // 4
    freqs = np.concatenate([np.arange(0, half, 2), np.arange(1, half, 2)])
    wave = 2.0 * math.pi / side * freqs

    def basis(cells):
        turn = (freqs[:, None] * cells[None, :]) % side
        angle = 2.0 * math.pi / side * turn
        cos, sin = np.cos(angle), np.sin(angle)
        return np.concatenate([cos[:quarter], sin[:quarter], cos[quarter:], sin[quarter:]])

    def slope(cells):
        turn = (freqs[:, None] * cells[None, :]) % side
        angle = 2.0 * math.pi / side * turn
        cos, sin = -wave[:, None] * np.sin(angle), wave[:, None] * np.cos(angle)
        return np.concatenate([cos[:quarter], sin[:quarter], cos[quarter:], sin[quarter:]])

    plain = basis(np.arange(half))
    even, odd = plain[:half], plain[half:]
    ring = np.concatenate([np.arange(rows + 1), np.zeros(PAD - 2, int), [side - 1]])
    used = np.ones(rows + PAD)
    used[rows + 1 : rows + PAD - 1] = 0.0
    plain_rows, slope_rows = (basis(ring) * used).T, (slope(ring) * used).T
    twice = np.repeat(wave.reshape(2, 1, quarter), 2, axis=1).reshape(-1) ** 2
    views = np.concatenate([plain_rows, slope_rows, plain_rows * twice, slope_rows * twice])
    up = np.concatenate([plain_rows, slope_rows]).T
    wave_sq = wave[:, None] ** 2 + wave[None, :] ** 2
    inverse = np.where(wave_sq > 0, 1.0 / np.where(wave_sq > 0, wave_sq, 1.0), 0.0)
    weight = np.where(freqs == 0, 1.0, 2.0)
    gain = AMPLITUDE * (np.sqrt(wave_sq) / PIVOT) / (1.0 + wave_sq / PIVOT**2)
    gain = gain * weight[:, None] * weight[None, :] / (side * side)
    sections = []
    for table in (even, odd, even.T, odd.T):
        sections.append(np.concatenate(split_np(np.ascontiguousarray(table)), axis=1))
    sections.extend(split_np(views))
    up_h, up_l = split_np(np.ascontiguousarray(up))
    lift = np.concatenate([up_h, up_h, up_l], axis=1)
    sections.append(np.concatenate([lift, np.zeros((side, side - lift.shape[1]), lift.dtype)], axis=1))
    waves = np.zeros((8, half))
    waves[:] = wave[None, :]
    return (
        np.concatenate(sections[2:4]),
        np.concatenate(sections[:2] + sections[4:]),
        np.concatenate([gain, gain * inverse, waves]).astype(np.float32),
    )


class Tables:
    def __init__(self, backs, packed, reals, side, ring):
        half = side // 2
        self.half = half
        self.ring = ring
        self.backs = backs
        self.packed = packed
        self.reals = reals
        self.lift_at = 2 * half + 8 * ring

    def fwd(self, par):
        half, at = self.half, par * self.half
        return self.packed[at : at + half, :half], self.packed[at : at + half, half:]

    def back(self, par):
        half, at = self.half, par * self.half
        return self.backs[at : at + half, :half], self.backs[at : at + half, half:]

    def views(self):
        at, count = 2 * self.half, 4 * self.ring
        return self.packed[at : at + count, :], self.packed[at + count : at + 2 * count, :]

    def lift(self, start, count):
        return self.packed[self.lift_at + start : self.lift_at + start + count, : 6 * self.ring]

    def gain(self, par, ypar):
        q = self.half // 2
        return self.reals[par * q : (par + 1) * q, ypar * q : (ypar + 1) * q]

    def gain_phi(self, par, ypar):
        q, half = self.half // 2, self.half
        return self.reals[half + par * q : half + (par + 1) * q, ypar * q : (ypar + 1) * q]

    def waves(self):
        q, half = self.half // 2, self.half
        row = self.reals[2 * half : 2 * half + 1, :]
        return row[:, :q], row[:, q:]


def mm(a, b):
    return jnp.dot(a, b, preferred_element_type=F32)


def split(a):
    high = a.astype(BF16)
    return high, (a - high.astype(F32)).astype(BF16)


def mm3(a, b):
    count = a[0].shape[0]
    both = mm(jnp.concatenate([a[0], a[1]], axis=0), b[0])
    return both[:count] + (both[count:] + mm(a[0], b[1]))


def turn_rows(a, step):
    return pltpu.roll(a, step % a.shape[0], 0)


def turn_lanes(a, step):
    return pltpu.roll(a, step % a.shape[1], 1)


def slope_lanes(a, waves, orient):
    q = a.shape[1] // 4
    parts = []
    for par in range(2):
        w = waves[par] * orient
        cos, sin = a[:, 2 * par * q : (2 * par + 1) * q], a[:, (2 * par + 1) * q : (2 * par + 2) * q]
        parts.extend([w * sin, -w * cos])
    return jnp.concatenate(parts, axis=1)


def place_of(me, k, n):
    return lax.rem(lax.bitwise_xor(me, k) - me + n, n)


def along_y_kernel(n, rows, side, *refs):
    half = side // 2
    blocks = refs[: n // 2]
    backs, out, fh, fl = refs[n // 2 :]
    tabs = Tables(backs, None, None, side, 0)
    me = lax.axis_index("gy")
    for i in range(n // 4):
        a, b = blocks[i][...], blocks[i + n // 4][...]
        place = place_of(me, 2 * i, n)
        sign = jnp.where(place < n // 2, 1.0, -1.0).astype(F32)
        off = pl.multiple_of(lax.rem(place, n // 2) // 2 * rows, rows)
        for par, v in ((0, a + b), (1, (a - b) * sign)):
            lo, hi = v[:, :half], v[:, half:]
            for ypar, w in ((0, lo + hi), (1, lo - hi)):
                h, l = split(w)
                fh[par, pl.ds(off, rows), ypar * half : (ypar + 1) * half] = h
                fl[par, pl.ds(off, rows), ypar * half : (ypar + 1) * half] = l
    for par in range(2):
        for ypar in range(2):
            cols = slice(ypar * half, (ypar + 1) * half)
            out[par, :, cols] = mm3((fh[par, :, cols], fl[par, :, cols]), tabs.back(ypar))


def field_kernel(n, rows, side, *refs):
    half, q = side // 2, side // 4
    ring = rows + PAD
    values, own, other, packed, reals = refs[:5]
    density_out, smooth_out, fields_out = refs[5:8]
    yh, yl, zh, zl = refs[8:]
    tabs = Tables(None, packed, reals, side, ring)

    odd = lax.rem(lax.axis_index("gy"), 2)
    for i in range(n // 4):
        place = jnp.where(odd == 1, (2 * i - 1) % (n // 2), 2 * i + 1)
        off = pl.multiple_of(place * rows, rows)
        sign = jnp.where(odd == 1, -1.0, 1.0).astype(F32) if i == 0 else 1.0
        rs = slice(i * rows, (i + 1) * rows)
        for par in range(2):
            yh[par, 2 * i * rows : (2 * i + 1) * rows, :], yl[par, 2 * i * rows : (2 * i + 1) * rows, :] = split(
                own[par, rs, :]
            )
            v = other[par, rs, :]
            h, l = split(v * sign if par else v)
            yh[par, pl.ds(off, rows), :] = h
            yl[par, pl.ds(off, rows), :] = l

    for par in range(2):
        for ypar in range(2):
            cols = slice(ypar * half, (ypar + 1) * half)
            x = mm3(tabs.fwd(par), (yh[par, :, cols], yl[par, :, cols]))
            g = tabs.gain_phi(par, ypar)
            for i in range(2):
                for j in range(2):
                    phi = x[i * q : (i + 1) * q, j * q : (j + 1) * q] * g
                    rs = slice(par * half + i * q, par * half + (i + 1) * q)
                    c0 = ypar * half + j * q
                    zh[rs, c0 : c0 + q], zl[rs, c0 : c0 + q] = split(phi)

    w = mm3(tabs.views(), (zh[...], zl[...]))
    ky = tabs.waves()
    ky_sq = jnp.concatenate([ky[0] * ky[0]] * 2 + [ky[1] * ky[1]] * 2, axis=1)
    phi, phi_x, base, base_x = [w[i * ring : (i + 1) * ring] for i in range(4)]
    base, base_x = base + ky_sq * phi, base_x + ky_sq * phi_x
    stack = jnp.concatenate([base, phi_x, slope_lanes(phi, ky, 1.0), base_x, slope_lanes(base, ky, 1.0)], axis=0)
    sh, sl = split(stack)
    e = mm3((sh[:, :half], sl[:, :half]), tabs.fwd(0))
    o = mm3((sh[:, half:], sl[:, half:]), tabs.fwd(1))
    fields = jnp.concatenate([e + o, e - o], axis=1)
    fields_out[...] = fields
    linear, shift_x, shift_y, slope_x, slope_y = [fields[i * ring : (i + 1) * ring] for i in range(5)]
    density = linear + GROWTH * linear * linear - (shift_x * slope_x + shift_y * slope_y)
    density_out[...] = density[:rows]

    weights = [values[i : i + 1, :] for i in range(9)]
    beside = {0: density, 1: turn_lanes(density, -1), -1: turn_lanes(density, 1)}
    smooth = jnp.zeros_like(density)
    for a in (-1, 0, 1):
        band = sum(weights[(a + 1) * 3 + b + 1] * beside[b] for b in (-1, 0, 1))
        smooth = smooth + (turn_rows(band, -a) if a else band)
    smooth_out[...] = smooth[:rows]


def adjoint_kernel(n, rows, side, *refs):
    half, q = side // 2, side // 4
    ring = rows + PAD
    values, counts, kinds, smooth_in, fields, density, backs, packed, reals = refs[:9]
    density_out = refs[9]
    outs = refs[10 : 10 + n]
    yh, yl, part, sem = refs[10 + n :]
    tabs = Tables(backs, packed, reals, side, ring)
    ky = tabs.waves()
    me = lax.axis_index("gy")
    leave = pltpu.make_async_copy(density, density_out, sem)
    leave.start()

    smooth = smooth_in[...]
    linear, shift_x, shift_y, slope_x, slope_y = [fields[i * ring : (i + 1) * ring, :] for i in range(5)]
    mean_v, one_v, two_v = [kinds[i * 8 : i * 8 + 1, :] for i in range(3)]
    rate = mean_v * jnp.exp(one_v * smooth + two_v * smooth * smooth)
    score = (counts[...] - rate) * (one_v + 2.0 * two_v * smooth)
    score = jnp.concatenate([score, jnp.zeros((PAD, side), F32)], axis=0)
    weights = [values[i : i + 1, :] for i in range(9)]
    beside = {0: score, 1: turn_lanes(score, 1), -1: turn_lanes(score, -1)}
    pulled = jnp.zeros_like(score)
    for a in (-1, 0, 1):
        band = sum(weights[(a + 1) * 3 + b + 1] * beside[b] for b in (-1, 0, 1))
        pulled = pulled + (turn_rows(band, a) if a else band)

    bars = jnp.concatenate(
        [
            pulled * (1.0 + 2.0 * GROWTH * linear),
            -pulled * slope_x,
            -pulled * slope_y,
            -pulled * shift_x,
            -pulled * shift_y,
        ],
        axis=0,
    )
    lo, hi = bars[:, :half], bars[:, half:]
    ye = mm3(split(lo + hi), tabs.back(0))
    yo = mm3(split(lo - hi), tabs.back(1))
    modes = jnp.concatenate([ye, yo], axis=1)
    m_lin, m_sx, m_sy, m_gx, m_gy = [modes[i * ring : (i + 1) * ring] for i in range(5)]
    to_base = m_lin + slope_lanes(m_gy, ky, -1.0)
    to_phi = slope_lanes(m_sy, ky, -1.0)
    pile = jnp.concatenate(
        [jnp.concatenate([to_base, to_phi], axis=1), jnp.concatenate([m_gx, m_sx], axis=1)], axis=0
    )
    ph, plow = split(pile)
    pile3 = jnp.concatenate([ph, plow, ph], axis=0)

    for par in range(2):
        for i in range(2):
            rs = slice(par * half + i * q, par * half + (i + 1) * q)
            x = mm(tabs.lift(rs.start, q), pile3)
            for ypar in range(2):
                g = tabs.gain(par, ypar)
                g_phi = tabs.gain_phi(par, ypar)
                for j in range(2):
                    c0 = ypar * half + j * q
                    d = g * x[:, c0 : c0 + q] + g_phi * x[:, side + c0 : side + c0 + q]
                    yh[par, i * q : (i + 1) * q, c0 : c0 + q], yl[par, i * q : (i + 1) * q, c0 : c0 + q] = split(d)
    e = mm3(tabs.back(0), (yh[0], yl[0]))
    o = mm3(tabs.back(1), (yh[1], yl[1]))
    part[0] = e + o
    part[1] = e - o
    for k in range(n):
        place = place_of(me, k, n)
        off = pl.multiple_of(lax.rem(place, n // 2) * rows, rows)
        outs[k][...] = part[place // (n // 2), pl.ds(off, rows), :]
    leave.wait()


def message_kernel(groups, capacity, rows, *refs):
    counts, noise, backs, depth = refs[:4]
    msgs = refs[4 : 4 + groups]
    noise_out, backs_out, classes, sems = refs[4 + groups :]
    mine = lax.axis_index("gx")
    head = pltpu.make_async_copy(depth, classes, sems.at[groups])
    head.start()
    copies = []
    for k in range(groups):
        start = lax.bitwise_xor(mine, k) * capacity
        copies.append(
            pltpu.make_async_copy(
                counts.at[pl.ds(start * rows, capacity * rows)], msgs[k].at[pl.ds(0, capacity * rows), :], sems.at[k]
            )
        )
    copies.append(pltpu.make_async_copy(noise, noise_out, sems.at[groups + 1]))
    copies.append(pltpu.make_async_copy(backs, backs_out, sems.at[groups + 2]))
    for copy in copies:
        copy.start()
    head.wait()
    for k in range(groups):
        start = lax.bitwise_xor(mine, k) * capacity
        for r in range(capacity):
            at = capacity * rows + r
            msgs[k][at : at + 1, :] = jnp.full((1, TC), classes[start + r], jnp.int32)
    for copy in copies:
        copy.wait()


def arrival_order(groups):
    first = [k for k in (2, 3, 1) if k < groups]
    return first + [k for k in range(groups) if k not in first]


def select_kernel(groups, capacity, rows, depths, *refs):
    msgs = dict(zip(arrival_order(groups), refs[:groups]))
    picks, values, counts_out, kinds_out = refs[groups:]
    side = counts_out.shape[1]

    def piece(k, r):
        at = capacity * rows + r
        return msgs[k][r * rows : (r + 1) * rows, :], msgs[k][at : at + 1, :]

    for t in range(side // TC):
        cols = slice(t * TC, (t + 1) * TC)
        pick = picks[:1, cols]
        cells, classes = piece(0, 0)
        for k in range(groups):
            for r in range(capacity):
                if k + r:
                    hit = pick == k * capacity + r
                    more, kind = piece(k, r)
                    cells = jnp.where(hit, more, cells)
                    classes = jnp.where(hit, kind, classes)
        counts_out[:, cols] = cells.astype(F32)
        for i in range(3):
            at = STENCIL_ROWS + i * depths
            value = values[at : at + 1, cols]
            for d in range(1, depths):
                value = jnp.where(classes == d, values[at + d : at + d + 1, cols], value)
            kinds_out[i * 8 : (i + 1) * 8, cols] = jnp.broadcast_to(value, (8, TC))


def table_kernel(capacity, count, *refs):
    small, (*tables, picks, values) = refs[: 5 + count], refs[5 + count : 7 + 2 * count]
    owner, stencil, *kinds, sems = refs[7 + 2 * count :]
    side = values.shape[1]
    mine = lax.axis_index("gx")
    copies = [
        pltpu.make_async_copy(a, b, sems.at[i])
        for i, (a, b) in enumerate(zip(small, (owner, stencil, *kinds, *tables)))
    ]
    for copy in copies:
        copy.start()
    for copy in copies[:5]:
        copy.wait()
    for t in range(owner.shape[0]):
        rank = jnp.int32(0)
        for t2 in range(t):
            rank = rank + (owner[t2] == owner[t]).astype(jnp.int32)
        pick = lax.bitwise_xor(owner[t], mine) * capacity + rank
        picks[:, t * TC : (t + 1) * TC] = jnp.full((8, TC), pick, jnp.int32)
    for i in range(stencil.shape[0]):
        values[i : i + 1, :] = jnp.full((1, side), stencil[i], F32)
    at = STENCIL_ROWS
    for kind in kinds:
        for d in range(kind.shape[0]):
            values[at : at + 1, :] = jnp.full((1, side), kind[d], F32)
            at += 1
    for copy in copies[5:]:
        copy.wait()


def in_hbm(value):
    return pltpu.with_memory_space_constraint(value, pltpu.HBM)


def last_kernel(count, *refs):
    parts = refs[:count]
    noise, packed, out = refs[count:]
    total = parts[0][...]
    for p in parts[1:]:
        total = total + p[...]
    half = total.shape[1] // 2
    tabs = Tables(None, packed, None, 2 * half, 0)
    sh, sl = split(total)
    e = mm3((sh[:, :half], sl[:, :half]), tabs.fwd(0))
    o = mm3((sh[:, half:], sl[:, half:]), tabs.fwd(1))
    out[:, :half] = e + o - noise[:, :half]
    out[:, half:] = e - o - noise[:, half:]


def local(n, groups, noise, stencil, mean_counts, bias_one, bias_two, owner, depth, counts):
    _, rows, side = noise.shape
    own = noise.reshape(rows, side)
    tiles = side // TC
    slots = counts.shape[1]
    capacity = slots // groups
    backs, packed, reals = [jnp.asarray(t) for t in make_tables(side, rows)]
    vmem = pl.BlockSpec(memory_space=VMEM)
    hbm = pl.BlockSpec(memory_space=pltpu.HBM)

    def swap(value, k, axis="gy", size=n):
        return lax.ppermute(value, axis, [(i, i ^ k) for i in range(size)])

    blocks = {}
    for k in range(n - 2, 0, -2):
        blocks[k] = swap(own, k)
    small = (owner.reshape(tiles), stencil, mean_counts, bias_one, bias_two)
    depths = mean_counts.shape[0]
    *msgs, blocks[0], backs = pl.pallas_call(
        functools.partial(message_kernel, groups, capacity, rows),
        out_shape=[VMEM((capacity * rows + 8, TC), jnp.int32)] * groups
        + [VMEM((rows, side), F32), VMEM(backs.shape, backs.dtype)],
        in_specs=[hbm] * 4,
        out_specs=[vmem] * (groups + 2),
        scratch_shapes=[pltpu.SMEM((slots,), jnp.int32), pltpu.SemaphoreType.DMA((groups + 3,))],
        compiler_params=pltpu.CompilerParams(vmem_limit_bytes=4 * MIB),
        name="messages",
    )(*[in_hbm(a) for a in (counts.reshape(slots * rows, TC), own, backs, depth.reshape(slots))])
    for k in range(groups - 1, 0, -1):
        msgs[k] = swap(msgs[k], k, "gx", groups)

    half = side // 2
    ring = rows + PAD
    cell = jax.ShapeDtypeStruct((rows, side), F32)
    along_y = pl.pallas_call(
        functools.partial(along_y_kernel, n, rows, side),
        out_shape=jax.ShapeDtypeStruct((2, half // 2, side), F32),
        in_specs=[vmem] * (n // 2 + 1),
        out_specs=vmem,
        scratch_shapes=[VMEM((2, half // 2, side), BF16)] * 2,
        compiler_params=pltpu.CompilerParams(vmem_limit_bytes=8 * MIB),
        name="along_y",
    )(*[blocks[k] for k in range(0, n, 2)], backs)
    other = swap(along_y, 1)
    packed, reals, _ = lax.optimization_barrier((packed, reals, along_y))
    small = (owner.reshape(tiles), stencil, mean_counts, bias_one, bias_two)
    depths = mean_counts.shape[0]
    packed, reals, picks, values = pl.pallas_call(
        functools.partial(table_kernel, capacity, 2),
        out_shape=[
            VMEM(packed.shape, packed.dtype),
            VMEM(reals.shape, reals.dtype),
            VMEM((8, side), jnp.int32),
            VMEM((STENCIL_ROWS + -(-3 * depths // 8) * 8, side), F32),
        ],
        in_specs=[hbm] * 7,
        out_specs=[vmem] * 4,
        scratch_shapes=[*[pltpu.SMEM(a.shape, a.dtype) for a in small], pltpu.SemaphoreType.DMA((7,))],
        compiler_params=pltpu.CompilerParams(vmem_limit_bytes=4 * MIB),
        cost_estimate=pl.CostEstimate(flops=20_000_000_000, bytes_accessed=1, transcendentals=0),
        name="tables",
    )(*[in_hbm(a) for a in (*small, packed, reals)])
    density, smooth, fields = pl.pallas_call(
        functools.partial(field_kernel, n, rows, side),
        out_shape=[VMEM((rows, side), F32), VMEM((rows, side), F32), VMEM((5 * ring, side), F32)],
        in_specs=[vmem] * 5,
        out_specs=[vmem] * 3,
        scratch_shapes=[
            *[VMEM((2, half, side), BF16)] * 2,
            *[VMEM((side, side), BF16)] * 2,
        ],
        compiler_params=pltpu.CompilerParams(vmem_limit_bytes=16 * MIB),
        name="fields",
    )(values, along_y, other, packed, reals)
    picks, smooth = lax.optimization_barrier((picks, smooth))
    picked, kinds = pl.pallas_call(
        functools.partial(select_kernel, groups, capacity, rows, depths),
        out_shape=[VMEM((rows, side), F32), VMEM((24, side), F32)],
        in_specs=[vmem] * (groups + 2),
        out_specs=[vmem] * 2,
        compiler_params=pltpu.CompilerParams(vmem_limit_bytes=4 * MIB),
        name="select",
    )(*[msgs[k] for k in arrival_order(groups)], picks, values)
    density, *parts = pl.pallas_call(
        functools.partial(adjoint_kernel, n, rows, side),
        out_shape=[cell] * (1 + n),
        in_specs=[vmem] * 9,
        out_specs=[hbm] + [vmem] * n,
        scratch_shapes=[
            *[VMEM((2, half, side), BF16)] * 2,
            VMEM((2, half, side), F32),
            pltpu.SemaphoreType.DMA,
        ],
        compiler_params=pltpu.CompilerParams(vmem_limit_bytes=16 * MIB),
        name="adjoint",
    )(values, picked, kinds, smooth, fields, density, backs, packed, reals)
    sums = {}
    for k in range(n - 2, -1, -2):
        sums[k] = parts[k] + swap(parts[k + 1], 1)
    pieces = [sums[0]] + [swap(sums[k], k) for k in range(n - 2, 0, -2)]
    gradient = pl.pallas_call(
        functools.partial(last_kernel, len(pieces)),
        out_shape=cell,
        in_specs=[vmem] * (len(pieces) + 2),
        out_specs=vmem,
        compiler_params=pltpu.CompilerParams(vmem_limit_bytes=8 * MIB),
        name="sum_and_rows",
    )(*pieces, blocks[0], packed)
    return (gradient.reshape(1, rows, side), density.reshape(1, rows, side))


def solution(mesh):
    return jax.shard_map(
        functools.partial(local, mesh.shape["gy"], mesh.shape["gx"]),
        mesh=mesh,
        in_specs=(
            P("gx", "gy", None),
            P(),
            P(),
            P(),
            P(),
            P("gy", "gx", None, None),
            P("gx", None, "gy"),
            P("gx", None, "gy", None, None),
        ),
        out_specs=(P("gx", "gy", None), P("gx", "gy", None)),
        check_vma=False,
    )
```
